128 devices in a mesh: sky: 128 (over y, z, x, core).
Axes of the slice: x: 4, y: 4, z: 4, core: 2. Of those that a mesh axis runs over, the one named last changes fastest.
Arguments:
- cutouts: float32 [16384, 128, 128], P('sky'), may hold values from -6 to 6
- coeffs: float32 [16384, 3], P('sky'), may hold values from -4 to 4
- weights: float32 [16384], P('sky'), may hold values from 0.2 to 2
- owners: int32 [16384, 1], P('sky'), may hold values from 0 to 127; in each aligned block of 128 rows (0 to 127, 128 to 255, ...) at most 2 rows name the same one
- positions: int32 [16384], P('sky'), may hold values from 0 to 15
- basis_rows: float32 [3, 41], replicated, may hold values from -1 to 1
- basis_cols: float32 [3, 41], replicated, may hold values from -1 to 1
- template: float32 [65536, 512], P('sky'), may hold values from -6 to 6
- detect_taps: float32 [41], replicated, may hold values from 0.01 to 0.05
Outputs:
- coadd: float32 [65536, 512], P('sky')
- detection: float32 [65536, 512], P('sky')
The draws below stay inside these ranges and needn't reach their ends.
Inputs may be any that keep to these rules, and one draw needn't show every extreme that they name: `owners`: of the 128 blocks of one device, at most 2 go to one patch; some device sends exactly 2 to some patch.
All inputs are finite; a program needn't handle non-finite values.
Results may differ from the reference program's by a relative error of at most 0.00011.
Values sent between devices are 32-bit elements; how exact they have to be, the bound alone decides.
No kernel may reach another device: no remote copies, remote signals or barrier semaphores. Data moves between devices by JAX's collectives and lax.ppermute only.
A program may use at most 256 MiB of HBM per device.

```python
import math
import jax
import jax.numpy as jnp
import numpy as np
from jax import lax

BLOCK = 128
SIDE = 4
TAPS = 41
TERMS = 3
BLOCKS_DEV = 128
POSITIONS = 16
PATCH = 512
OWNERS = 128
BLOCKS = 16384
CAPACITY = 2


def set_ends(drawn, own_key, least, top_value):
    dims = drawn.shape
    place = [jax.random.randint(jax.random.fold_in(own_key, axis), (), 0, dims[axis]) for axis in range(len(dims))]
    drawn = drawn.at[tuple(place)].set(least)
    longest = dims.index(max(dims))
    place[longest] = (place[longest] + 1) % dims[longest]
    return drawn.at[tuple(place)].set(top_value)


def levels(own_key, dims, split, least, top_value):
    gain, own = 1.0, jax.random.fold_in(own_key, 6)
    for axis_at, parts in split:
        draws = jnp.exp(jax.random.uniform(jax.random.fold_in(own, axis_at), (parts,), jnp.float32, least / len(split), top_value / len(split)))
        gain = gain * jnp.repeat(draws, dims[axis_at] // parts).reshape([-1 if axis == axis_at else 1 for axis in range(len(dims))])
    return gain


def routed_block(key, own, number, rows, count, top, limit, skew):
    order = jax.random.permutation(key, count)
    packed, common = portions_of(count, rows * top, limit, skew, True), portions_of(count, rows * top, limit, skew, False)
    places = jnp.arange(count)

    def named(sizes, turn):
        used = int((sizes > 0).sum())
        fixed = max(1, used // 4)
        shifted = fixed + (places - fixed + turn * (used - fixed)) % max(1, count - fixed)
        return jnp.zeros((count,), jnp.int32).at[order[jnp.where(places < fixed, places, shifted)]].set(jnp.asarray(sizes, jnp.int32))

    sizes = jnp.where(number % 4 == 0, named(packed, number // 4), named(common, number - number // 4 - 1))
    mixed = jax.random.permutation(jax.random.fold_in(own, 3), count)
    giver, receiver = mixed[0:count // 2 * 2:2], mixed[1:count // 2 * 2:2]
    room = jnp.minimum(sizes[giver] - 1, limit - sizes[receiver]) // 2
    room = jnp.where((giver == order[0]) | (receiver == order[0]) | (sizes[receiver] == 0), 0, jnp.maximum(room, 0))
    shifted = jax.random.randint(jax.random.fold_in(own, 4), (count // 2,), 0, 1 << 20) % (room + 1)
    sizes = sizes.at[giver].add(-shifted).at[receiver].add(shifted)
    labels = jnp.searchsorted(jnp.cumsum(sizes), jnp.arange(rows * top), side="right").astype(jnp.int32)
    listing = labels.reshape(top, rows).T
    listing = listing[jax.random.permutation(jax.random.fold_in(own, 1), rows)]
    turn = jax.random.randint(jax.random.fold_in(own, 2), (rows, 1), 0, top)
    return jnp.take_along_axis(listing, (jnp.arange(top)[None, :] + turn) % top, axis=1)


def portions_of(amount, total, reach, slope, full):
    weights = [(1 << 20) // math.isqrt(standing ** slope) + 1 for standing in range(1, amount + 1)]
    largest = reach if full else min(reach, max(-(-total // amount), total * weights[0] // sum(weights)))
    least = 1 if total - largest >= amount - 1 else 0
    counts, rest = [largest] + [least] * (amount - 1), total - largest - least * (amount - 1)
    while rest > 0:
        free = [i for i in range(1, amount) if counts[i] < largest] or [i for i in range(1, amount) if counts[i] < reach]
        pool, left = sum([weights[i] for i in free]), rest
        for i in free:
            extra = min(reach - counts[i], max(1, left * weights[i] // pool), rest)
            counts[i] = counts[i] + extra
            rest = rest - extra
    return np.array(counts)


def normal_values(stream_key, dims, spread, bound, shards=(), held_as=jnp.bfloat16):
    result = spread * jax.random.normal(stream_key, dims, jnp.float32)
    if shards:
        result = result * levels(stream_key, dims, shards, -0.22, 0.18)
    return jnp.clip(result, -bound, bound).astype(held_as)


def setup_inputs(seed: int = 0) -> dict:
    splits = jax.random.split(jax.random.key(seed), 10)
    cutouts = normal_values(splits[0], (BLOCKS, BLOCK, BLOCK), 1.0, 6.0, ((0, 128),), jnp.float32)
    coeffs = normal_values(splits[1], (BLOCKS, TERMS), 1.0, 4.0, ((0, 128),), jnp.float32)
    weights = jnp.clip(jnp.exp(math.log(2.0) - 2.3025851 * jax.random.uniform(splits[2], (BLOCKS,), jnp.float32) ** levels(splits[2], (BLOCKS,), ((0, 128),), -0.2, 0.2)), 0.2, 2.0)
    owners_keys = jax.random.split(jax.random.fold_in(splits[3], 1), BLOCKS // BLOCKS_DEV)
    owners_turns = jax.random.permutation(jax.random.fold_in(splits[3], 3), BLOCKS // BLOCKS_DEV)
    owners = jax.vmap(lambda own, number: routed_block(jax.random.fold_in(splits[3], 2), own, number, BLOCKS_DEV, OWNERS, 1, CAPACITY, 2))(owners_keys, owners_turns).reshape((BLOCKS, 1))
    positions = set_ends(jax.random.randint(splits[4], (BLOCKS,), 0, POSITIONS), jax.random.fold_in(splits[4], 1), 0, POSITIONS - 1).astype(jnp.int32)
    basis_rows = normal_values(splits[5], (TERMS, TAPS), TAPS ** -0.5, 1.0, (), jnp.float32)
    basis_cols = normal_values(splits[6], (TERMS, TAPS), TAPS ** -0.5, 1.0, (), jnp.float32)
    template = normal_values(splits[7], (OWNERS * PATCH, PATCH), 1.0, 6.0, ((0, 128),), jnp.float32)
    detect_taps = jnp.clip(jax.random.uniform(splits[8], (TAPS,), jnp.float32, 0.01, 0.05), 0.01, 0.05)
    return {"cutouts": cutouts, "coeffs": coeffs, "weights": weights, "owners": owners, "positions": positions, "basis_rows": basis_rows, "basis_cols": basis_cols, "template": template, "detect_taps": detect_taps}


EXACT = lax.Precision.HIGHEST


def band(taps, rows, cols, offset):
    count = taps.shape[-1]
    lag = jnp.arange(cols, dtype=jnp.int32)[None, :] - jnp.arange(rows, dtype=jnp.int32)[:, None] + offset
    inside = (lag >= 0) & (lag < count)
    picked = jnp.take(taps, jnp.clip(lag, 0, count - 1), axis=-1)
    return jnp.where(inside, picked, jnp.zeros_like(picked))


def match_blocks(blocks, coefs, row_mats, col_mats):
    total = jnp.zeros(blocks.shape, jnp.float32)
    for term in range(row_mats.shape[0]):
        rowed = jnp.einsum("ij,njl->nil", row_mats[term], blocks, precision=EXACT)
        both = jnp.einsum("nil,ml->nim", rowed, col_mats[term], precision=EXACT)
        total = total + coefs[:, term][:, None, None] * both
    return total


def to_blocks(image):
    groups = image.shape[0] // PATCH
    return image.reshape(groups, SIDE, BLOCK, SIDE, BLOCK).transpose(0, 1, 3, 2, 4).reshape(groups * SIDE * SIDE, BLOCK, BLOCK)


def from_blocks(stacked):
    groups = stacked.shape[0] // (SIDE * SIDE)
    return stacked.reshape(groups, SIDE, SIDE, BLOCK, BLOCK).transpose(0, 1, 3, 2, 4).reshape(groups * PATCH, PATCH)


def reference(cutouts, coeffs, weights, owners, positions, basis_rows, basis_cols, template, detect_taps):
    half = (TAPS - 1) // 2
    row_mats = band(basis_rows, BLOCK, BLOCK, half)
    col_mats = band(basis_cols, BLOCK, BLOCK, half)
    target = (owners[:, 0] * POSITIONS + positions).astype(jnp.int32)
    pieces = (cutouts.reshape(OWNERS, BLOCKS_DEV, BLOCK, BLOCK), coeffs.reshape(OWNERS, BLOCKS_DEV, TERMS),
              weights.reshape(OWNERS, BLOCKS_DEV), target.reshape(OWNERS, BLOCKS_DEV))

    def accumulate(numer, piece):
        blocks, coefs, block_weights, slots = piece
        matched = match_blocks(blocks, coefs, row_mats, col_mats)
        return numer.at[slots].add(block_weights[:, None, None] * matched), None

    numer, _ = lax.scan(accumulate, jnp.zeros((OWNERS * POSITIONS, BLOCK, BLOCK), jnp.float32), pieces)
    wsum = jax.ops.segment_sum(weights, target, num_segments=OWNERS * POSITIONS)
    stacked = (to_blocks(template) + numer) / (1.0 + wsum[:, None, None])
    coadd = from_blocks(stacked)
    total_rows = coadd.shape[0]
    padded = jnp.pad(coadd, ((half, half), (0, 0)))
    rowed = jnp.zeros_like(coadd)
    for offset in range(TAPS):
        rowed = rowed + detect_taps[offset] * padded[offset:offset + total_rows, :]
    padded_cols = jnp.pad(rowed, ((0, 0), (half, half)))
    detection = jnp.zeros_like(coadd)
    for offset in range(TAPS):
        detection = detection + detect_taps[offset] * padded_cols[:, offset:offset + PATCH]
    return coadd, detection
```

```python
import functools

import jax
import jax.numpy as jnp
from jax import lax
from jax.experimental import pallas as pl
from jax.experimental.pallas import tpu as pltpu
from jax.sharding import PartitionSpec as P

BLOCK = 128
SIDE = 4
PATCH = 512
PLACES = 16
TERMS = 3
TAPS = 41
HALF = 20
EDGE = 24
GROUP = 8
CHUNKS = (64, 64)
DEPTH = 1024
WIDE = 256
VMEM = 40 * 1024 * 1024
F32 = jnp.float32
BF16 = jnp.bfloat16


def halves(x):
    high = x.astype(BF16)
    return high, (x - high.astype(F32)).astype(BF16)


def dot(a, b):
    return jnp.dot(a, b, preferred_element_type=F32)


def lagged(rows, cols, sign, offset, tap):
    lag = (
        lax.broadcasted_iota(jnp.int32, (rows, cols), 1)
        - lax.broadcasted_iota(jnp.int32, (rows, cols), 0)
    ) * sign + offset

    def body(t, made):
        return jnp.where(lag == t, tap(t), made)

    return lax.fori_loop(0, TAPS, body, jnp.zeros((rows, cols), F32))


def match_kernel(
    first, coeffs_ref, weights_ref, rows_ref, cols_ref, x_ref, o_ref, rr, cc, y_ref
):
    step = pl.program_id(0)

    @pl.when(step == 0)
    def _():
        wide = TERMS * BLOCK
        for k in range(TERMS):
            at = k * BLOCK
            high, low = halves(lagged(BLOCK, BLOCK, 1, HALF, lambda t: rows_ref[k, t]))
            rr[:, at : at + BLOCK] = high
            rr[:, wide + at : wide + at + BLOCK] = high
            rr[:, 2 * wide + at : 2 * wide + at + BLOCK] = low
            high, low = halves(lagged(BLOCK, BLOCK, -1, HALF, lambda t: cols_ref[k, t]))
            cc[0:BLOCK, at : at + BLOCK] = high
            cc[BLOCK : 2 * BLOCK, at : at + BLOCK] = high
            cc[2 * BLOCK : 3 * BLOCK, at : at + BLOCK] = low

    high, low = halves(x_ref[...].reshape(GROUP * BLOCK, BLOCK))
    y_ref[...] = dot(jnp.concatenate([high, low, high], axis=1), cc[...])
    flat = o_ref.reshape(BLOCK * GROUP, BLOCK)
    for pair in range(GROUP // 2):
        both = []
        for b in (2 * pair, 2 * pair + 1):
            at = first + step * GROUP + b
            weight = weights_ref[at]
            both.append(
                jnp.concatenate(
                    [
                        y_ref[b * BLOCK : (b + 1) * BLOCK, k * BLOCK : (k + 1) * BLOCK]
                        * (weight * coeffs_ref[at, k])
                        for k in range(TERMS)
                    ],
                    axis=0,
                )
            )
        high, low = halves(jnp.concatenate(both, axis=1))
        out = dot(rr[...], jnp.concatenate([high, low, high], axis=0))
        flat[pl.ds(2 * pair, BLOCK, stride=GROUP), :] = out[:, :BLOCK]
        flat[pl.ds(2 * pair + 1, BLOCK, stride=GROUP), :] = out[:, BLOCK:]


def match(first, count, coeffs, weights, basis_rows, basis_cols, cutouts):
    smem = pl.BlockSpec(memory_space=pltpu.SMEM)
    return pl.pallas_call(
        functools.partial(match_kernel, first),
        grid=(count // GROUP,),
        in_specs=[
            smem,
            smem,
            smem,
            smem,
            pl.BlockSpec((GROUP, BLOCK, BLOCK), lambda i: (first // GROUP + i, 0, 0)),
        ],
        out_specs=pl.BlockSpec((BLOCK, GROUP, BLOCK), lambda i: (0, i, 0)),
        out_shape=jax.ShapeDtypeStruct((BLOCK, count, BLOCK), F32),
        scratch_shapes=[
            pltpu.VMEM((BLOCK, 3 * TERMS * BLOCK), BF16),
            pltpu.VMEM((3 * BLOCK, TERMS * BLOCK), BF16),
            pltpu.VMEM((GROUP * BLOCK, TERMS * BLOCK), F32),
        ],
        compiler_params=pltpu.CompilerParams(vmem_limit_bytes=VMEM),
        cost_estimate=pl.CostEstimate(
            flops=count * 2 * 6 * TERMS * BLOCK**3,
            bytes_accessed=count * 8 * BLOCK * BLOCK,
            transcendentals=0,
        ),
    )(coeffs, weights, basis_rows, basis_cols, cutouts)


def combine_kernel(slots, carried, *refs):
    if carried:
        prior_ref, ids_ref, x_ref, o_ref = refs
    else:
        ids_ref, x_ref, o_ref = refs

    @pl.when(pl.program_id(0) == 0)
    def _():
        o_ref[...] = prior_ref[...] if carried else jnp.zeros_like(o_ref)

    high, low = halves(x_ref[...])
    both = jnp.concatenate([high, low], axis=1)
    ids = ids_ref[0]
    place = lax.broadcasted_iota(jnp.int32, (WIDE, DEPTH), 0)

    def body(m, carry):
        at = pl.multiple_of(m * WIDE, WIDE)
        marks = jnp.where(place == ids - at, 1.0, 0.0).astype(BF16)
        sums = dot(marks, both)
        o_ref[pl.ds(at, WIDE), :] += sums[:, :BLOCK] + sums[:, BLOCK:]
        return carry

    lax.fori_loop(0, slots // WIDE, body, 0)


def combine(prior, ids, rows, slots):
    steps = rows.shape[0] // DEPTH
    whole = pl.BlockSpec((slots, BLOCK), lambda i: (0, 0))
    extra = [] if prior is None else [prior]
    return pl.pallas_call(
        functools.partial(combine_kernel, slots, prior is not None),
        grid=(steps,),
        in_specs=[whole] * len(extra)
        + [
            pl.BlockSpec((1, 1, DEPTH), lambda i: (i, 0, 0)),
            pl.BlockSpec((DEPTH, BLOCK), lambda i: (i, 0)),
        ],
        out_specs=whole,
        out_shape=jax.ShapeDtypeStruct((slots, BLOCK), F32),
        compiler_params=pltpu.CompilerParams(vmem_limit_bytes=VMEM),
        cost_estimate=pl.CostEstimate(
            flops=4 * slots * rows.shape[0] * BLOCK,
            bytes_accessed=rows.shape[0] * BLOCK * 4,
            transcendentals=0,
        ),
    )(*extra, ids.reshape(steps, 1, DEPTH), rows)


def coadd_kernel(divisor_ref, sums_ref, template_ref, coadd_ref, head_ref, tail_ref):
    flat = sums_ref.reshape(BLOCK * PLACES, BLOCK)
    for r in range(SIDE):
        for c in range(SIDE):
            place = r * SIDE + c
            numer = flat[pl.ds(place, BLOCK, stride=PLACES), :]
            rows, cols = slice(r * BLOCK, (r + 1) * BLOCK), slice(c * BLOCK, (c + 1) * BLOCK)
            coadd_ref[rows, cols] = (template_ref[rows, cols] + numer) / divisor_ref[place]
    head_ref[...] = coadd_ref[:EDGE, :]
    tail_ref[...] = coadd_ref[PATCH - EDGE :, :]


def make_coadd(divisor, sums, template):
    vmem = pl.BlockSpec(memory_space=pltpu.VMEM)
    edge = jax.ShapeDtypeStruct((EDGE, PATCH), F32)
    return pl.pallas_call(
        coadd_kernel,
        in_specs=[pl.BlockSpec(memory_space=pltpu.SMEM), vmem, vmem],
        out_specs=[vmem, vmem, vmem],
        out_shape=[jax.ShapeDtypeStruct((PATCH, PATCH), F32), edge, edge],
        compiler_params=pltpu.CompilerParams(vmem_limit_bytes=VMEM),
    )(divisor, sums, template)


def bands_kernel(taps_ref, down_ref, along_ref):
    tap = lambda t: taps_ref[t]
    high, low = halves(lagged(BLOCK, 2 * BLOCK, 1, HALF - EDGE, tap))
    down_ref[...] = jnp.concatenate([high, high, low], axis=1)
    for part in range(4):
        high, low = halves(
            lagged(BLOCK, 2 * BLOCK, -1, HALF - BLOCK + part * BLOCK, tap)
        )
        for copy, piece in enumerate((high, high, low)):
            at = copy * PATCH + part * BLOCK
            along_ref[at : at + BLOCK, :] = piece


def make_bands(taps):
    vmem = pl.BlockSpec(memory_space=pltpu.VMEM)
    return pl.pallas_call(
        bands_kernel,
        in_specs=[pl.BlockSpec(memory_space=pltpu.SMEM)],
        out_specs=[vmem, vmem],
        out_shape=[
            jax.ShapeDtypeStruct((BLOCK, 6 * BLOCK), BF16),
            jax.ShapeDtypeStruct((3 * PATCH, 2 * BLOCK), BF16),
        ],
        compiler_params=pltpu.CompilerParams(vmem_limit_bytes=VMEM),
    )(taps)


def detect_kernel(down_ref, along_ref, before_ref, coadd_ref, after_ref, o_ref, pad, row):
    spare = pad.shape[0] - PATCH - 2 * EDGE
    pad[:EDGE, :] = before_ref[...]
    pad[EDGE : EDGE + PATCH, :] = coadd_ref[...]
    pad[EDGE + PATCH : 2 * EDGE + PATCH, :] = after_ref[...]
    pad[2 * EDGE + PATCH :, :] = jnp.zeros((spare, PATCH), F32)
    row[:, :BLOCK] = jnp.zeros((PATCH, BLOCK), F32)
    row[:, BLOCK + PATCH :] = jnp.zeros((PATCH, BLOCK), F32)
    for r in range(SIDE):
        high, low = halves(pad[r * BLOCK : (r + 2) * BLOCK, :])
        row[r * BLOCK : (r + 1) * BLOCK, BLOCK : BLOCK + PATCH] = dot(
            down_ref[...], jnp.concatenate([high, low, high], axis=0)
        )
    for h in range(2):
        high, low = halves(row[:, h * 2 * BLOCK : h * 2 * BLOCK + PATCH])
        o_ref[:, h * 2 * BLOCK : (h + 1) * 2 * BLOCK] = dot(
            jnp.concatenate([high, low, high], axis=1), along_ref[...]
        )


def detect(down, along, before, coadd, after):
    vmem = pl.BlockSpec(memory_space=pltpu.VMEM)
    return pl.pallas_call(
        detect_kernel,
        in_specs=[vmem] * 5,
        out_specs=vmem,
        out_shape=jax.ShapeDtypeStruct((PATCH, PATCH), F32),
        scratch_shapes=[
            pltpu.VMEM((PATCH + BLOCK, PATCH), F32),
            pltpu.VMEM((PATCH, PATCH + 2 * BLOCK), F32),
        ],
        compiler_params=pltpu.CompilerParams(vmem_limit_bytes=VMEM),
    )(down, along, before, coadd, after)


def local(
    cutouts, coeffs, weights, owners, positions, basis_rows, basis_cols, template, detect_taps
):
    peers = lax.axis_size("sky")
    me = lax.axis_index("sky")
    slots = peers * PLACES
    mine = (owners[:, 0] * PLACES + positions).astype(F32)
    known = lax.all_gather(jnp.stack([mine, weights]), "sky")
    ids = known[:, 0, :].astype(jnp.int32)
    sums, first = None, 0
    for count in CHUNKS:
        turned = match(first, count, coeffs, weights, basis_rows, basis_cols, cutouts)
        rows = lax.all_to_all(turned, "sky", split_axis=0, concat_axis=0, tiled=True)
        sums = combine(
            sums, ids[:, first : first + count], rows.reshape(peers * count, BLOCK), slots
        )
        first += count
    hits = ids[None] == (me * PLACES + jnp.arange(PLACES, dtype=jnp.int32))[:, None, None]
    divisor = 1.0 + jnp.sum(jnp.where(hits, known[None, :, 1, :], 0.0), axis=(1, 2))
    down, along = make_bands(detect_taps)
    back = lax.all_to_all(
        sums.reshape(peers, PLACES, BLOCK), "sky", split_axis=0, concat_axis=0, tiled=True
    )
    coadd, head, tail = make_coadd(divisor, back, template)
    before = lax.ppermute(tail, "sky", [(i, i + 1) for i in range(peers - 1)])
    after = lax.ppermute(head, "sky", [(i + 1, i) for i in range(peers - 1)])
    return coadd, detect(down, along, before, coadd, after)


def solution(mesh):
    placed = (
        P("sky", None, None),
        P("sky", None),
        P("sky"),
        P("sky", None),
        P("sky"),
        P(),
        P(),
        P("sky", None),
        P(),
    )
    return jax.shard_map(
        local,
        mesh=mesh,
        in_specs=placed,
        out_specs=(P("sky", None), P("sky", None)),
        check_vma=False,
    )
```

```python
import functools

import jax
import jax.numpy as jnp
from jax import lax
from jax.experimental import pallas as pl
from jax.experimental.pallas import tpu as pltpu
from jax.sharding import PartitionSpec as P

BLOCK = 128
SIDE = 4
PATCH = 512
PLACES = 16
TERMS = 3
TAPS = 41
HALF = 20
EDGE = 24
GROUP = 8
WIDE = 256
STRIPE = 24
FIRST = 16
VMEM = 56 * 1024 * 1024
F32 = jnp.float32
BF16 = jnp.bfloat16


def halves(x):
    high = x.astype(BF16)
    return high, (x - high.astype(F32)).astype(BF16)


def dot(a, b):
    return jnp.dot(a, b, preferred_element_type=F32)


def toeplitz(taps, offset):
    lane = lax.broadcasted_iota(jnp.int32, (BLOCK, BLOCK), 1)
    lag = lane - lax.broadcasted_iota(jnp.int32, (BLOCK, BLOCK), 0) + offset
    slant = pltpu.roll(jnp.broadcast_to(taps, (8, BLOCK)), 0, 1, stride=1, stride_axis=0)
    turned = jnp.concatenate(
        [pltpu.roll(slant, (at - offset) % BLOCK, 1) for at in range(0, BLOCK, 8)], axis=0
    )
    return jnp.where((lag >= 0) & (lag < TAPS), turned, 0.0)


def as_column(row):
    same = lax.broadcasted_iota(jnp.int32, (BLOCK, BLOCK), 0) == lax.broadcasted_iota(
        jnp.int32, (BLOCK, BLOCK), 1
    )
    return jnp.sum(jnp.where(same, row, jnp.zeros_like(row)), axis=1, keepdims=True)


def match_kernel(steps, order_ref, ids_ref, coeffs_ref, weights_ref, rows_ref, cols_ref, *refs):
    x_refs = refs[:GROUP]
    o_ref, rr, cc, scale, lhs = refs[GROUP:]
    step = pl.program_id(0)
    wide = TERMS * BLOCK

    @pl.when(step == 0)
    def _():
        scale[0] = jnp.zeros((BLOCK, BLOCK), F32)
        scale[0, 0:TERMS, 0:TAPS] = rows_ref[...]
        scale[0, 8 : 8 + TERMS, 0:TAPS] = cols_ref[...]
        for k in range(TERMS):
            at = k * BLOCK
            high, low = halves(toeplitz(scale[0, k : k + 1, :], HALF))
            rr[at : at + BLOCK, :] = jnp.concatenate([high, high, low], axis=1)
            high, low = halves(toeplitz(scale[0, 8 + k : 9 + k, :], HALF).T)
            cc[at : at + BLOCK, :] = jnp.concatenate([high, low], axis=1)
            cc[wide + at : wide + at + BLOCK, :] = jnp.concatenate(
                [high, jnp.zeros_like(low)], axis=1
            )
        for k in range(TERMS):
            column = as_column(coeffs_ref[k : k + 1, :] * weights_ref[...])
            scale[k] = jnp.broadcast_to(column, (BLOCK, BLOCK))

    @pl.when(step < steps)
    def _():
        for pair in range(GROUP // 2):
            both = jnp.concatenate([x_refs[2 * pair][0], x_refs[2 * pair + 1][0]], axis=1)
            high, low = halves(both)
            rowed = dot(rr[...], jnp.concatenate([high, low, high], axis=0))
            for part in range(2):
                b = 2 * pair + part
                at = order_ref[step * GROUP + b]
                for k in range(TERMS):
                    piece = rowed[k * BLOCK : (k + 1) * BLOCK, part * BLOCK : (part + 1) * BLOCK]
                    high, low = halves(piece * scale[k, pl.ds(at, 1), :])
                    lhs[b * BLOCK : (b + 1) * BLOCK, k * BLOCK : (k + 1) * BLOCK] = high
                    lhs[
                        b * BLOCK : (b + 1) * BLOCK, wide + k * BLOCK : wide + (k + 1) * BLOCK
                    ] = low
        out = dot(lhs[...], cc[...])
        out = out[:, :BLOCK] + out[:, BLOCK:]
        flat = o_ref.reshape(BLOCK * GROUP, BLOCK)
        for b in range(GROUP):
            flat[pl.ds(b, BLOCK, stride=GROUP), :] = out[b * BLOCK : (b + 1) * BLOCK, :]

    @pl.when(step == steps)
    def _():
        blank = jnp.zeros((GROUP - 2, BLOCK), F32)
        note = jnp.concatenate([ids_ref[...], weights_ref[...], blank], axis=0)
        o_ref[...] = jnp.broadcast_to(note[None], o_ref.shape)


def match(order, noted, ids, coeffs, weights, basis_rows, basis_cols, cutouts):
    count = order.shape[0]
    steps = count // GROUP
    vmem = pl.BlockSpec(memory_space=pltpu.VMEM)

    def pick(b):
        def block(i, order_ref):
            return (order_ref[jnp.minimum(i, steps - 1) * GROUP + b], 0, 0)

        return pl.BlockSpec((1, BLOCK, BLOCK), block)

    return pl.pallas_call(
        functools.partial(match_kernel, steps),
        grid_spec=pltpu.PrefetchScalarGridSpec(
            num_scalar_prefetch=1,
            grid=(steps + noted,),
            in_specs=[vmem] * 5 + [pick(b) for b in range(GROUP)],
            out_specs=pl.BlockSpec((BLOCK, GROUP, BLOCK), lambda i, order_ref: (0, i, 0)),
            scratch_shapes=[
                pltpu.VMEM((TERMS * BLOCK, 3 * BLOCK), BF16),
                pltpu.VMEM((2 * TERMS * BLOCK, 2 * BLOCK), BF16),
                pltpu.VMEM((TERMS, BLOCK, BLOCK), F32),
                pltpu.VMEM((GROUP * BLOCK, 2 * TERMS * BLOCK), BF16),
            ],
        ),
        out_shape=jax.ShapeDtypeStruct((BLOCK, count + noted * GROUP, BLOCK), F32),
        compiler_params=pltpu.CompilerParams(vmem_limit_bytes=VMEM),
        cost_estimate=pl.CostEstimate(
            flops=count * 2 * 6 * TERMS * BLOCK**3,
            bytes_accessed=count * 8 * BLOCK * BLOCK,
            transcendentals=0,
        ),
    )(order, ids, coeffs, weights, basis_rows, basis_cols, *[cutouts] * GROUP)


def combine_kernel(last, me_ref, base_ref, turns_ref, ids_ref, x_ref, *refs):
    prior_ref = refs[0] if last else None
    o_ref, acc, both, held, got = refs[-5:]
    step = pl.program_id(0)
    steps = held.shape[0]

    def fetch(at):
        place = pl.ds(pl.multiple_of(at * GROUP, GROUP), GROUP)
        return pltpu.make_async_copy(x_ref.at[:, place, :], held.at[at], got.at[at])

    @pl.when(step == 0)
    def _():
        for at in range(steps):
            fetch(at).start()
        acc[...] = prior_ref[...] if last else jnp.zeros_like(acc)

    fetch(step).wait()
    depth = both.shape[0]
    high, low = halves(held[step].reshape(depth, BLOCK))
    both[:, :BLOCK] = high
    both[:, BLOCK:] = low
    ids = ids_ref[step]
    place = lax.broadcasted_iota(jnp.int32, (WIDE, depth), 0).astype(F32).astype(BF16)

    def body(m, carry):
        at = pl.multiple_of(base_ref[step] + m * 2 * WIDE, PLACES)
        marks = []
        for half in range(2):
            near = ids - (at + half * WIDE).astype(F32)
            near = jnp.clip(near, -1.0, float(WIDE)).astype(BF16)
            marks.append(jnp.where(place == near, jnp.ones_like(place), jnp.zeros_like(place)))
        sums = dot(jnp.concatenate(marks, axis=0), both[...])
        acc[pl.ds(at, 2 * WIDE), :] += sums[:, :BLOCK] + sums[:, BLOCK:]
        return carry

    lax.fori_loop(0, turns_ref[step], body, 0)

    @pl.when(step == steps - 1)
    def _():
        if not last:
            o_ref[...] = acc[...]
            return
        peers = o_ref.shape[0]
        slots = peers * PLACES
        o_ref[:, :PLACES, :] = acc[:slots, :].reshape(peers, PLACES, BLOCK)

        @pl.when(me_ref[0] < BLOCK // 2)
        def _():
            later = acc[PLACES : slots + PLACES, :].reshape(peers, PLACES, BLOCK)
            o_ref[:, PLACES:, :] = later[:, : STRIPE - PLACES, :]

        @pl.when(me_ref[0] >= BLOCK // 2)
        def _():
            sooner = acc[: slots - PLACES, :].reshape(peers - 1, PLACES, BLOCK)
            o_ref[0:1, PLACES:, :] = jnp.zeros((1, STRIPE - PLACES, BLOCK), F32)
            o_ref[1:, PLACES:, :] = sooner[:, 2 * PLACES - STRIPE :, :]


def tiled(ids):
    peers, count = ids.shape
    steps = count // GROUP
    tiles = ids.reshape(peers, steps, GROUP).transpose(1, 0, 2).reshape(steps, 1, peers * GROUP)
    base = jnp.min(tiles, axis=(1, 2)).astype(jnp.int32) // PLACES * PLACES
    turns = (jnp.max(tiles, axis=(1, 2)).astype(jnp.int32) - base) // (2 * WIDE) + 1
    return base, turns, tiles


def combine(me, tiles, rows, prior=None):
    steps, _, depth = tiles[2].shape
    peers = depth // GROUP
    room = peers * PLACES + 2 * WIDE
    last = prior is not None
    out = (peers, STRIPE, BLOCK) if last else (room, BLOCK)
    vmem = pl.BlockSpec(memory_space=pltpu.VMEM)
    return pl.pallas_call(
        functools.partial(combine_kernel, last),
        grid_spec=pltpu.PrefetchScalarGridSpec(
            num_scalar_prefetch=3,
            grid=(steps,),
            in_specs=[vmem, pl.BlockSpec(memory_space=pl.ANY)] + [vmem] * last,
            out_specs=pl.BlockSpec(out, lambda i, *_: (0,) * len(out)),
            scratch_shapes=[
                pltpu.VMEM((room, BLOCK), F32),
                pltpu.VMEM((depth, 2 * BLOCK), BF16),
                pltpu.VMEM((steps, peers, GROUP, BLOCK), F32),
                pltpu.SemaphoreType.DMA((steps,)),
            ],
        ),
        out_shape=jax.ShapeDtypeStruct(out, F32),
        compiler_params=pltpu.CompilerParams(vmem_limit_bytes=VMEM),
        cost_estimate=pl.CostEstimate(
            flops=4 * 2 * WIDE * steps * depth * BLOCK,
            bytes_accessed=steps * depth * BLOCK * 4,
            transcendentals=0,
        ),
    )(me.reshape(1), *tiles, rows, *([prior] if last else []))


def bands_kernel(taps_ref, down_ref, along_ref, row):
    row[...] = jnp.zeros_like(row)
    row[0:1, 0:TAPS] = taps_ref[...]
    taps = row[0:1, :]
    for part in range(2):
        high, low = halves(toeplitz(taps, HALF - EDGE + part * BLOCK))
        for copy, piece in enumerate((high, high, low)):
            at = (2 * copy + part) * BLOCK
            down_ref[:, at : at + BLOCK] = piece
    along_ref[...] = jnp.zeros_like(along_ref)
    for part in range(3):
        high, low = halves(toeplitz(taps, HALF + (part - 1) * BLOCK).T)
        for copy, piece in enumerate((high, high, low)):
            for half in range(2):
                at = copy * PATCH + (part + half) * BLOCK
                along_ref[at : at + BLOCK, half * BLOCK : (half + 1) * BLOCK] = piece


def make_bands(taps):
    vmem = pl.BlockSpec(memory_space=pltpu.VMEM)
    return pl.pallas_call(
        bands_kernel,
        in_specs=[vmem],
        out_specs=[vmem, vmem],
        out_shape=[
            jax.ShapeDtypeStruct((BLOCK, 6 * BLOCK), BF16),
            jax.ShapeDtypeStruct((3 * PATCH, 2 * BLOCK), BF16),
        ],
        scratch_shapes=[pltpu.VMEM((8, BLOCK), F32)],
        compiler_params=pltpu.CompilerParams(vmem_limit_bytes=VMEM),
    )(taps.reshape(1, TAPS))


def finish_kernel(
    divisor_ref,
    sums_ref,
    template_ref,
    above_ref,
    below_ref,
    down_ref,
    along_ref,
    coadd_ref,
    detection_ref,
    pad,
    row,
):
    flat = sums_ref.reshape(BLOCK * STRIPE, BLOCK)
    spare = pad.shape[0] - PATCH - 2 * EDGE
    pad[2 * EDGE + PATCH :, :] = jnp.zeros((spare, PATCH), F32)
    row[:, :BLOCK] = jnp.zeros((PATCH, BLOCK), F32)
    row[:, BLOCK + PATCH :] = jnp.zeros((PATCH, BLOCK), F32)
    for c in range(SIDE):
        cols = slice(c * BLOCK, (c + 1) * BLOCK)
        numer = flat[pl.ds((BLOCK - EDGE) * STRIPE + STRIPE - SIDE + c, EDGE, stride=STRIPE), :]
        pad[:EDGE, cols] = (above_ref[:, cols] + numer) / divisor_ref[PLACES + c]
        numer = flat[pl.ds(PLACES + c, EDGE, stride=STRIPE), :]
        pad[EDGE + PATCH : 2 * EDGE + PATCH, cols] = (
            below_ref[:, cols] + numer
        ) / divisor_ref[PLACES + SIDE + c]
        for r in range(SIDE):
            place = r * SIDE + c
            numer = flat[pl.ds(place, BLOCK, stride=STRIPE), :]
            rows = slice(r * BLOCK, (r + 1) * BLOCK)
            made = (template_ref[rows, cols] + numer) / divisor_ref[place]
            coadd_ref[rows, cols] = made
            pad[EDGE + r * BLOCK : EDGE + (r + 1) * BLOCK, cols] = made
    for r in range(SIDE):
        high, low = halves(pad[r * BLOCK : (r + 2) * BLOCK, :])
        row[r * BLOCK : (r + 1) * BLOCK, BLOCK : BLOCK + PATCH] = dot(
            down_ref[...], jnp.concatenate([high, low, high], axis=0)
        )
    for h in range(2):
        high, low = halves(row[:, h * 2 * BLOCK : h * 2 * BLOCK + PATCH])
        detection_ref[:, h * 2 * BLOCK : (h + 1) * 2 * BLOCK] = dot(
            jnp.concatenate([high, low, high], axis=1), along_ref[...]
        )


def finish(divisor, sums, template, above, below, down, along):
    vmem = pl.BlockSpec(memory_space=pltpu.VMEM)
    image = jax.ShapeDtypeStruct((PATCH, PATCH), F32)
    return pl.pallas_call(
        finish_kernel,
        in_specs=[pl.BlockSpec(memory_space=pltpu.SMEM)] + [vmem] * 6,
        out_specs=[vmem, vmem],
        out_shape=[image, image],
        scratch_shapes=[
            pltpu.VMEM((PATCH + BLOCK, PATCH), F32),
            pltpu.VMEM((PATCH, PATCH + 2 * BLOCK), F32),
        ],
        compiler_params=pltpu.CompilerParams(vmem_limit_bytes=VMEM),
    )(divisor, sums, template, above, below, down, along)


def ranks(keys):
    before = jnp.arange(keys.shape[-1])
    before = before[None, :] < before[:, None]
    mine, other = keys[..., :, None], keys[..., None, :]
    return jnp.sum(((other < mine) | ((other == mine) & before)).astype(jnp.int32), axis=-1)


def argsorted(keys):
    spots = jnp.arange(keys.shape[-1], dtype=jnp.int32)
    hits = ranks(keys)[..., None, :] == spots[:, None]
    return jnp.sum(jnp.where(hits, spots, 0), axis=-1)


def in_order(keys):
    spots = jnp.arange(keys.shape[-1], dtype=jnp.int32)
    hits = ranks(keys)[..., None, :] == spots[:, None]
    return jnp.sum(jnp.where(hits, keys[..., None, :], 0.0), axis=-1)


def local(
    cutouts, coeffs, weights, owners, positions, basis_rows, basis_cols, template, detect_taps
):
    peers = lax.axis_size("sky")
    me = lax.axis_index("sky")
    blocks = cutouts.shape[0]
    mine = (owners[:, 0] * PLACES + positions).astype(F32)
    order = argsorted(mine)
    given = (
        mine.reshape(1, blocks),
        coeffs.T,
        weights.reshape(1, blocks),
        basis_rows,
        basis_cols,
        cutouts,
    )
    early = match(order[:FIRST], True, *given)
    early = lax.all_to_all(early, "sky", split_axis=0, concat_axis=0, tiled=True)
    late = match(order[FIRST:], False, *given)
    late = lax.all_to_all(late, "sky", split_axis=0, concat_axis=0, tiled=True)
    known, template_late = lax.optimization_barrier((early[:, FIRST:, :], template))
    ids = known[:, 0, :]
    down, along = make_bands(detect_taps)
    above = lax.ppermute(
        template_late[PATCH - EDGE :], "sky", [(i, i + 1) for i in range(peers - 1)]
    )
    below = lax.ppermute(template_late[:EDGE], "sky", [(i + 1, i) for i in range(peers - 1)])
    wanted = jnp.concatenate(
        [
            jnp.arange(PLACES),
            jnp.arange(-SIDE, 0),
            jnp.arange(PLACES, PLACES + SIDE),
        ]
    )
    hits = ids[None] == (me * PLACES + wanted).astype(F32)[:, None, None]
    divisor = 1.0 + jnp.sum(jnp.where(hits, known[None, :, 1, :], 0.0), axis=(1, 2))
    ordered = in_order(ids)
    sums = combine(me, tiled(ordered[:, :FIRST]), early)
    late, sums, down, along, divisor, above, below, tiles = lax.optimization_barrier(
        (late, sums, down, along, divisor, above, below, tiled(ordered[:, FIRST:]))
    )
    sums = combine(me, tiles, late, sums)
    back = lax.all_to_all(sums, "sky", split_axis=0, concat_axis=0, tiled=True)
    return tuple(finish(divisor, back, template, above, below, down, along))


def solution(mesh):
    placed = (
        P("sky", None, None),
        P("sky", None),
        P("sky"),
        P("sky", None),
        P("sky"),
        P(),
        P(),
        P("sky", None),
        P(),
    )
    return jax.shard_map(
        local,
        mesh=mesh,
        in_specs=placed,
        out_specs=(P("sky", None), P("sky", None)),
        check_vma=False,
    )
```

```python
import functools

import jax
import jax.numpy as jnp
from jax import lax
from jax.experimental import pallas as pl
from jax.experimental.pallas import tpu as pltpu
from jax.sharding import PartitionSpec as P

BLOCK = 128
SIDE = 4
PATCH = 512
PLACES = 16
TERMS = 3
TAPS = 41
HALF = 20
EDGE = 24
GROUP = 8
WIDE = 256
STRIPE = PLACES + SIDE
FIRST = 16
NOTES = 2
BANDS = ((0, 56, 0, 80), (56, 16, 32, 64), (72, 56, 48, 80))
VMEM = 56 * 1024 * 1024
LEAN = 24 * 1024 * 1024
F32 = jnp.float32
BF16 = jnp.bfloat16


def halves(x):
    high = x.astype(BF16)
    return high, (x - high.astype(F32)).astype(BF16)


def dot(a, b):
    return jnp.dot(a, b, preferred_element_type=F32)


def toeplitz(taps, offset):
    lane = lax.broadcasted_iota(jnp.int32, (BLOCK, BLOCK), 1)
    lag = lane - lax.broadcasted_iota(jnp.int32, (BLOCK, BLOCK), 0) + offset
    slant = pltpu.roll(jnp.broadcast_to(taps, (8, BLOCK)), 0, 1, stride=1, stride_axis=0)
    turned = jnp.concatenate(
        [pltpu.roll(slant, (at - offset) % BLOCK, 1) for at in range(0, BLOCK, 8)], axis=0
    )
    return jnp.where((lag >= 0) & (lag < TAPS), turned, 0.0)


def as_column(row):
    same = lax.broadcasted_iota(jnp.int32, (BLOCK, BLOCK), 0) == lax.broadcasted_iota(
        jnp.int32, (BLOCK, BLOCK), 1
    )
    return jnp.sum(jnp.where(same, row, jnp.zeros_like(row)), axis=1, keepdims=True)


def match_kernel(noted, order_ref, ids_ref, coeffs_ref, weights_ref, rows_ref, cols_ref, *refs):
    x_refs = refs[:GROUP]
    o_ref, rr, cc, scale, lhs = refs[GROUP:]
    step = pl.program_id(0)
    wide = TERMS * BLOCK

    @pl.when(step == 0)
    def _():
        scale[0] = jnp.zeros((BLOCK, BLOCK), F32)
        scale[0, 0:TERMS, 0:TAPS] = rows_ref[...]
        scale[0, 8 : 8 + TERMS, 0:TAPS] = cols_ref[...]
        for k in range(TERMS):
            at = k * BLOCK
            rows = toeplitz(scale[0, k : k + 1, :], HALF)
            for first, count, start, reach in BANDS:
                high, low = halves(rows)
                into = TERMS * first + k * count
                picked = slice(first, first + count)
                seen = slice(start, start + reach)
                blank = jnp.zeros((count, 2 * BLOCK - 3 * reach), BF16)
                rr[into : into + count, :] = jnp.concatenate(
                    [high[picked, seen], high[picked, seen], low[picked, seen], blank], axis=1
                )
            high, low = halves(toeplitz(scale[0, 8 + k : 9 + k, :], HALF).T)
            cc[at : at + BLOCK, :] = jnp.concatenate([high, low], axis=1)
            cc[wide + at : wide + at + BLOCK, :] = jnp.concatenate(
                [high, jnp.zeros_like(low)], axis=1
            )
        for k in range(TERMS):
            column = as_column(coeffs_ref[k : k + 1, :] * weights_ref[...])
            scale[k] = jnp.broadcast_to(column, (BLOCK, BLOCK))
        if noted:
            for row, note in enumerate((ids_ref, weights_ref)):
                o_ref[pl.ds(FIRST + row, BLOCK, stride=FIRST + NOTES), :] = jnp.broadcast_to(
                    note[...], (BLOCK, BLOCK)
                )

    for pair in range(GROUP // 2):
        both = jnp.concatenate([x_refs[2 * pair][0], x_refs[2 * pair + 1][0]], axis=1)
        high, low = halves(both)
        rowed = []
        for first, count, start, reach in BANDS:
            seen = slice(start, start + reach)
            spare = high[: 2 * BLOCK - 3 * reach]
            rowed.append(
                dot(
                    rr[TERMS * first : TERMS * (first + count), :],
                    jnp.concatenate([high[seen], low[seen], high[seen], spare], axis=0),
                )
            )
        for part in range(2):
            b = 2 * pair + part
            at = order_ref[step * GROUP + b]
            for k in range(TERMS):
                piece = jnp.concatenate(
                    [
                        made[k * band[1] : (k + 1) * band[1], part * BLOCK : (part + 1) * BLOCK]
                        for made, band in zip(rowed, BANDS)
                    ],
                    axis=0,
                )
                high_, low_ = halves(piece * scale[k, pl.ds(at, 1), :])
                lhs[b * BLOCK : (b + 1) * BLOCK, k * BLOCK : (k + 1) * BLOCK] = high_
                lhs[
                    b * BLOCK : (b + 1) * BLOCK, wide + k * BLOCK : wide + (k + 1) * BLOCK
                ] = low_
    out = dot(lhs[...], cc[...])
    out = out[:, :BLOCK] + out[:, BLOCK:]
    if noted:
        stride, first = FIRST + NOTES, step * GROUP
        flat = o_ref
    else:
        stride, first = GROUP, 0
        flat = o_ref.reshape(BLOCK * GROUP, BLOCK)
    for b in range(GROUP):
        flat[pl.ds(first + b, BLOCK, stride=stride), :] = out[b * BLOCK : (b + 1) * BLOCK, :]


def match(order, noted, ids, coeffs, weights, basis_rows, basis_cols, cutouts):
    count = order.shape[0]
    steps = count // GROUP
    vmem = pl.BlockSpec(memory_space=pltpu.VMEM)

    def pick(b):
        def block(i, order_ref):
            return (order_ref[i * GROUP + b], 0, 0)

        return pl.BlockSpec((1, BLOCK, BLOCK), block)

    return pl.pallas_call(
        functools.partial(match_kernel, noted),
        grid_spec=pltpu.PrefetchScalarGridSpec(
            num_scalar_prefetch=1,
            grid=(steps,),
            in_specs=[vmem] * 5 + [pick(b) for b in range(GROUP)],
            out_specs=vmem
            if noted
            else pl.BlockSpec((BLOCK, GROUP, BLOCK), lambda i, order_ref: (0, i, 0)),
            scratch_shapes=[
                pltpu.VMEM((TERMS * BLOCK, 2 * BLOCK), BF16),
                pltpu.VMEM((2 * TERMS * BLOCK, 2 * BLOCK), BF16),
                pltpu.VMEM((TERMS, BLOCK, BLOCK), F32),
                pltpu.VMEM((GROUP * BLOCK, 2 * TERMS * BLOCK), BF16),
            ],
        ),
        out_shape=jax.ShapeDtypeStruct(
            (BLOCK * (count + NOTES), BLOCK) if noted else (BLOCK, count, BLOCK), F32
        ),
        compiler_params=pltpu.CompilerParams(vmem_limit_bytes=VMEM),
        cost_estimate=pl.CostEstimate(
            flops=count * 2 * 6 * TERMS * BLOCK**3,
            bytes_accessed=count * 8 * BLOCK * BLOCK,
            transcendentals=0,
        ),
    )(order, ids, coeffs, weights, basis_rows, basis_cols, *[cutouts] * GROUP)


def combine_kernel(last, scalars_ref, ids_ref, x_ref, *refs):
    step = pl.program_id(0)
    steps, _, depth = ids_ref.shape
    if last:
        prior_ref, o_ref, acc, held, got = refs
    else:
        o_ref, acc = refs

    def fetch(at):
        place = pl.ds(pl.multiple_of(at * GROUP, GROUP), GROUP)
        return pltpu.make_async_copy(x_ref.at[:, place, :], held.at[at], got.at[at])

    @pl.when(step == 0)
    def _():
        if last:
            for at in range(steps):
                fetch(at).start()
        acc[...] = prior_ref[...] if last else jnp.zeros_like(acc)

    if last:
        fetch(step).wait()
        rows = held[step].reshape(depth, BLOCK)
    else:
        peers = depth // GROUP
        rows = jnp.concatenate(
            [
                x_ref[pl.ds(step * GROUP + b, peers, stride=FIRST + NOTES), :]
                for b in range(GROUP)
            ],
            axis=0,
        )
    high, low = halves(rows)
    both = jnp.concatenate([high, low], axis=1)
    ids = ids_ref[step]
    spot = lax.broadcasted_iota(jnp.int32, (WIDE, depth), 0)

    def body(m, carry):
        at = pl.multiple_of(scalars_ref[1 + step] + m * WIDE, PLACES)
        near = (ids - at.astype(F32)).astype(jnp.int32)
        marks = jnp.where(spot == near, 1.0, 0.0).astype(BF16)
        sums = dot(marks, both)
        acc[pl.ds(at + PLACES, WIDE), :] += sums[:, :BLOCK] + sums[:, BLOCK:]
        return carry

    body(0, 0)
    lax.fori_loop(1, scalars_ref[1 + steps + step], body, 0)

    @pl.when(step == steps - 1)
    def _():
        if not last:
            o_ref[...] = acc[...]
            return
        peers = o_ref.shape[0] // STRIPE
        for place in range(PLACES):
            o_ref[pl.ds(place, peers, stride=STRIPE), :] = acc[
                pl.ds(PLACES + place, peers, stride=PLACES), :
            ]
        for below in (False, True):

            @pl.when((scalars_ref[0] < BLOCK // 2) == below)
            def _():
                first = 2 * PLACES if below else PLACES - SIDE
                for c in range(SIDE):
                    o_ref[pl.ds(PLACES + c, peers, stride=STRIPE), :] = acc[
                        pl.ds(first + c, peers, stride=PLACES), :
                    ]


def combine(me, ids, rows, prior=None):
    last = prior is not None
    peers, count = ids.shape
    steps = count // GROUP
    depth = peers * GROUP
    tiles = ids.reshape(peers, steps, GROUP).transpose((1, 0, 2) if last else (1, 2, 0))
    base = jnp.min(tiles, axis=(1, 2)).astype(jnp.int32) // PLACES * PLACES
    turns = (jnp.max(tiles, axis=(1, 2)).astype(jnp.int32) - base) // WIDE + 1
    room = PLACES + peers * PLACES + WIDE
    out = (peers * STRIPE if last else room, BLOCK)
    vmem = pl.BlockSpec(memory_space=pltpu.VMEM)
    return pl.pallas_call(
        functools.partial(combine_kernel, last),
        grid_spec=pltpu.PrefetchScalarGridSpec(
            num_scalar_prefetch=1,
            grid=(steps,),
            in_specs=[vmem, pl.BlockSpec(memory_space=pl.ANY), vmem] if last else [vmem, vmem],
            out_specs=vmem,
            scratch_shapes=[pltpu.VMEM((room, BLOCK), F32)]
            + [
                pltpu.VMEM((steps, peers, GROUP, BLOCK), F32),
                pltpu.SemaphoreType.DMA((steps,)),
            ]
            * last,
        ),
        out_shape=jax.ShapeDtypeStruct(out, F32),
        compiler_params=pltpu.CompilerParams(vmem_limit_bytes=LEAN),
        cost_estimate=pl.CostEstimate(
            flops=4 * WIDE * steps * depth * BLOCK,
            bytes_accessed=steps * depth * BLOCK * 4,
            transcendentals=0,
        ),
    )(
        jnp.concatenate([me.reshape(1), base, turns]),
        tiles.reshape(steps, 1, depth),
        rows,
        *([prior] if last else []),
    )


def bands_kernel(taps_ref, down_ref, along_ref, row):
    row[...] = jnp.zeros_like(row)
    row[0:1, 0:TAPS] = taps_ref[...]
    taps = row[0:1, :]
    for part in range(2):
        high, low = halves(toeplitz(taps, HALF - EDGE + part * BLOCK))
        for copy, piece in enumerate((high, high, low)):
            at = (2 * copy + part) * BLOCK
            down_ref[:, at : at + BLOCK] = piece
    along_ref[...] = jnp.zeros_like(along_ref)
    for part in range(3):
        high, low = halves(toeplitz(taps, HALF + (part - 1) * BLOCK).T)
        for copy, piece in enumerate((high, high, low)):
            for half in range(2):
                at = copy * PATCH + (part + half) * BLOCK
                along_ref[at : at + BLOCK, half * BLOCK : (half + 1) * BLOCK] = piece


def make_bands(taps):
    vmem = pl.BlockSpec(memory_space=pltpu.VMEM)
    return pl.pallas_call(
        bands_kernel,
        in_specs=[vmem],
        out_specs=[vmem, vmem],
        out_shape=[
            jax.ShapeDtypeStruct((BLOCK, 6 * BLOCK), BF16),
            jax.ShapeDtypeStruct((3 * PATCH, 2 * BLOCK), BF16),
        ],
        scratch_shapes=[pltpu.VMEM((8, BLOCK), F32)],
        compiler_params=pltpu.CompilerParams(vmem_limit_bytes=LEAN),
    )(taps.reshape(1, TAPS))


def finish_kernel(
    divisor_ref,
    sums_ref,
    template_ref,
    above_ref,
    below_ref,
    down_ref,
    along_ref,
    coadd_ref,
    detection_ref,
    pad,
    row,
):
    flat = sums_ref
    spare = pad.shape[0] - PATCH - 2 * EDGE
    pad[2 * EDGE + PATCH :, :] = jnp.zeros((spare, PATCH), F32)
    row[:, :BLOCK] = jnp.zeros((PATCH, BLOCK), F32)
    row[:, BLOCK + PATCH :] = jnp.zeros((PATCH, BLOCK), F32)
    for c in range(SIDE):
        cols = slice(c * BLOCK, (c + 1) * BLOCK)
        numer = flat[pl.ds((BLOCK - EDGE) * STRIPE + PLACES + c, EDGE, stride=STRIPE), :]
        pad[:EDGE, cols] = (above_ref[:, cols] + numer) / divisor_ref[PLACES + c]
        numer = flat[pl.ds(PLACES + c, EDGE, stride=STRIPE), :]
        pad[EDGE + PATCH : 2 * EDGE + PATCH, cols] = (
            below_ref[:, cols] + numer
        ) / divisor_ref[PLACES + SIDE + c]
        for r in range(SIDE):
            place = r * SIDE + c
            numer = flat[pl.ds(place, BLOCK, stride=STRIPE), :]
            rows = slice(r * BLOCK, (r + 1) * BLOCK)
            made = (template_ref[rows, cols] + numer) / divisor_ref[place]
            coadd_ref[rows, cols] = made
            pad[EDGE + r * BLOCK : EDGE + (r + 1) * BLOCK, cols] = made
    for r in range(SIDE):
        high, low = halves(pad[r * BLOCK : (r + 2) * BLOCK, :])
        row[r * BLOCK : (r + 1) * BLOCK, BLOCK : BLOCK + PATCH] = dot(
            down_ref[...], jnp.concatenate([high, low, high], axis=0)
        )
    for h in range(2):
        high, low = halves(row[:, h * 2 * BLOCK : h * 2 * BLOCK + PATCH])
        detection_ref[:, h * 2 * BLOCK : (h + 1) * 2 * BLOCK] = dot(
            jnp.concatenate([high, low, high], axis=1), along_ref[...]
        )


def finish(divisor, sums, template, above, below, down, along):
    vmem = pl.BlockSpec(memory_space=pltpu.VMEM)
    image = jax.ShapeDtypeStruct((PATCH, PATCH), F32)
    return pl.pallas_call(
        finish_kernel,
        in_specs=[pl.BlockSpec(memory_space=pltpu.SMEM)] + [vmem] * 6,
        out_specs=[vmem, vmem],
        out_shape=[image, image],
        scratch_shapes=[
            pltpu.VMEM((PATCH + BLOCK, PATCH), F32),
            pltpu.VMEM((PATCH, PATCH + 2 * BLOCK), F32),
        ],
        compiler_params=pltpu.CompilerParams(vmem_limit_bytes=LEAN),
    )(divisor, sums, template, above, below, down, along)


def ranks(keys):
    before = jnp.arange(keys.shape[-1])
    before = before[None, :] < before[:, None]
    mine, other = keys[..., :, None], keys[..., None, :]
    return jnp.sum(((other < mine) | ((other == mine) & before)).astype(jnp.int32), axis=-1)


def argsorted(keys):
    spots = jnp.arange(keys.shape[-1], dtype=jnp.int32)
    hits = ranks(keys)[..., None, :] == spots[:, None]
    return jnp.sum(jnp.where(hits, spots, 0), axis=-1)


def in_order(keys):
    spots = jnp.arange(keys.shape[-1], dtype=jnp.int32)
    hits = ranks(keys)[..., None, :] == spots[:, None]
    return jnp.sum(jnp.where(hits, keys[..., None, :], 0.0), axis=-1)


def local(
    cutouts, coeffs, weights, owners, positions, basis_rows, basis_cols, template, detect_taps
):
    peers = lax.axis_size("sky")
    me = lax.axis_index("sky")
    blocks = cutouts.shape[0]
    mine = (owners[:, 0] * PLACES + positions).astype(F32)
    order = argsorted(mine)
    given = (
        mine.reshape(1, blocks),
        coeffs.T,
        weights.reshape(1, blocks),
        basis_rows,
        basis_cols,
        cutouts,
    )
    early = match(order[:FIRST], True, *given)
    early = early.reshape(peers, -1, NOTES, BLOCK)
    early = lax.all_to_all(early, "sky", split_axis=0, concat_axis=0, tiled=True)
    late = match(order[FIRST:], False, *given)
    late = lax.all_to_all(late, "sky", split_axis=0, concat_axis=0, tiled=True)
    known, template_late = lax.optimization_barrier((early[:, -1], template))
    ids = known[:, 0, :]
    down, along = make_bands(detect_taps)
    above = lax.ppermute(
        template_late[PATCH - EDGE :], "sky", [(i, i + 1) for i in range(peers - 1)]
    )
    below = lax.ppermute(template_late[:EDGE], "sky", [(i + 1, i) for i in range(peers - 1)])
    wanted = jnp.concatenate(
        [
            jnp.arange(PLACES),
            jnp.arange(-SIDE, 0),
            jnp.arange(PLACES, PLACES + SIDE),
        ]
    )
    hits = ids[None] == (me * PLACES + wanted).astype(F32)[:, None, None]
    divisor = 1.0 + jnp.sum(jnp.where(hits, known[None, :, 1, :], 0.0), axis=(1, 2))
    ordered = in_order(ids)
    sums = combine(me, ordered[:, :FIRST], early.reshape(-1, BLOCK))
    late, sums, down, along, divisor, above, below = lax.optimization_barrier(
        (late, sums, down, along, divisor, above, below)
    )
    sums = combine(me, ordered[:, FIRST:], late, sums)
    sums = sums.reshape(peers, STRIPE // SIDE, SIDE, BLOCK)
    back = lax.all_to_all(sums, "sky", split_axis=0, concat_axis=0, tiled=True)
    back = back.reshape(peers * STRIPE, BLOCK)
    return tuple(finish(divisor, back, template, above, below, down, along))


def solution(mesh):
    placed = (
        P("sky", None, None),
        P("sky", None),
        P("sky"),
        P("sky", None),
        P("sky"),
        P(),
        P(),
        P("sky", None),
        P(),
    )
    return jax.shard_map(
        local,
        mesh=mesh,
        in_specs=placed,
        out_specs=(P("sky", None), P("sky", None)),
        check_vma=False,
    )
```

```python
import functools

import jax
import jax.numpy as jnp
from jax import lax
from jax.experimental import pallas as pl
from jax.experimental.pallas import tpu as pltpu
from jax.sharding import PartitionSpec as P

BLOCK = 128
SIDE = 4
PATCH = 512
PLACES = 16
TERMS = 3
TAPS = 41
HALF = 20
EDGE = 24
GROUP = 8
WIDE = 256
LATE_WIDE = 400
STRIPE = PLACES + SIDE
FIRST = 24
NOTES = 2
BANDS = ((0, 56, 0, 80), (56, 16, 32, 64), (72, 56, 48, 80))
VMEM = 56 * 1024 * 1024
LEAN = 24 * 1024 * 1024
F32 = jnp.float32
BF16 = jnp.bfloat16


def halves(x):
    high = x.astype(BF16)
    return high, (x - high.astype(F32)).astype(BF16)


def dot(a, b):
    return jnp.dot(a, b, preferred_element_type=F32)


def toeplitz(taps, offset):
    lane = lax.broadcasted_iota(jnp.int32, (BLOCK, BLOCK), 1)
    lag = lane - lax.broadcasted_iota(jnp.int32, (BLOCK, BLOCK), 0) + offset
    slant = pltpu.roll(jnp.broadcast_to(taps, (8, BLOCK)), 0, 1, stride=1, stride_axis=0)
    turned = jnp.concatenate(
        [pltpu.roll(slant, (at - offset) % BLOCK, 1) for at in range(0, BLOCK, 8)], axis=0
    )
    return jnp.where((lag >= 0) & (lag < TAPS), turned, 0.0)


def as_column(row):
    same = lax.broadcasted_iota(jnp.int32, (BLOCK, BLOCK), 0) == lax.broadcasted_iota(
        jnp.int32, (BLOCK, BLOCK), 1
    )
    return jnp.sum(jnp.where(same, row, jnp.zeros_like(row)), axis=1, keepdims=True)


def prepare(coeffs_ref, weights_ref, rows_ref, cols_ref, rr, cc, scale):
    wide = TERMS * BLOCK
    scale[0] = jnp.zeros((BLOCK, BLOCK), F32)
    scale[0, 0:TERMS, 0:TAPS] = rows_ref[...]
    scale[0, 8 : 8 + TERMS, 0:TAPS] = cols_ref[...]
    for k in range(TERMS):
        at = k * BLOCK
        high, low = halves(toeplitz(scale[0, k : k + 1, :], HALF))
        for first, count, start, reach in BANDS:
            into = TERMS * first + k * count
            picked = slice(first, first + count)
            seen = slice(start, start + reach)
            blank = jnp.zeros((count, 2 * BLOCK - 3 * reach), BF16)
            rr[into : into + count, :] = jnp.concatenate(
                [high[picked, seen], high[picked, seen], low[picked, seen], blank], axis=1
            )
        high, low = halves(toeplitz(scale[0, 8 + k : 9 + k, :], HALF).T)
        cc[at : at + BLOCK, :] = jnp.concatenate([high, low], axis=1)
        cc[wide + at : wide + at + BLOCK, :] = jnp.concatenate(
            [high, jnp.zeros_like(low)], axis=1
        )
    for k in range(TERMS):
        column = as_column(coeffs_ref[k : k + 1, :] * weights_ref[...])
        scale[k] = jnp.broadcast_to(column, (BLOCK, BLOCK))


def filtered(blocks, spots, rr, cc, scale, lhs):
    wide = TERMS * BLOCK
    for pair in range(GROUP // 2):
        high, low = halves(jnp.concatenate(blocks[2 * pair : 2 * pair + 2], axis=1))
        rowed = []
        for first, count, start, reach in BANDS:
            seen = slice(start, start + reach)
            spare = high[: 2 * BLOCK - 3 * reach]
            rowed.append(
                dot(
                    rr[TERMS * first : TERMS * (first + count), :],
                    jnp.concatenate([high[seen], low[seen], high[seen], spare], axis=0),
                )
            )
        for part in range(2):
            b = 2 * pair + part
            rows = slice(b * BLOCK, (b + 1) * BLOCK)
            for k in range(TERMS):
                piece = jnp.concatenate(
                    [
                        made[k * band[1] : (k + 1) * band[1], part * BLOCK : (part + 1) * BLOCK]
                        for made, band in zip(rowed, BANDS)
                    ],
                    axis=0,
                )
                upper, lower = halves(piece * scale[k, pl.ds(spots[b], 1), :])
                lhs[rows, k * BLOCK : (k + 1) * BLOCK] = upper
                lhs[rows, wide + k * BLOCK : wide + (k + 1) * BLOCK] = lower
    out = dot(lhs[...], cc[...])
    return out[:, :BLOCK] + out[:, BLOCK:]


def spread(flat, out):
    for b in range(GROUP):
        flat[pl.ds(b, BLOCK, stride=GROUP), :] = out[b * BLOCK : (b + 1) * BLOCK, :]


FILTER_SCRATCH = [
    pltpu.VMEM((TERMS * BLOCK, 2 * BLOCK), BF16),
    pltpu.VMEM((2 * TERMS * BLOCK, 2 * BLOCK), BF16),
    pltpu.VMEM((TERMS, BLOCK, BLOCK), F32),
    pltpu.VMEM((GROUP * BLOCK, 2 * TERMS * BLOCK), BF16),
]


def early_kernel(
    owners_in,
    positions_in,
    coeffs_in,
    weights_in,
    rows_in,
    cols_in,
    x_ref,
    o_ref,
    owners_ref,
    positions_ref,
    coeffs_ref,
    weights_ref,
    rows_ref,
    cols_ref,
    small,
    rr,
    cc,
    scale,
    lhs,
    held,
    made,
    note,
    got,
    sent,
):
    steps = FIRST // GROUP
    fetches = [
        pltpu.make_async_copy(
            x_ref.at[t * GROUP : (t + 1) * GROUP], held.at[t * GROUP : (t + 1) * GROUP], got.at[t]
        )
        for t in range(steps)
    ]
    smalls = [
        pltpu.make_async_copy(source, into, small.at[i])
        for i, (source, into) in enumerate(
            (
                (owners_in, owners_ref),
                (positions_in, positions_ref),
                (coeffs_in, coeffs_ref),
                (weights_in, weights_ref),
                (rows_in, rows_ref),
                (cols_in, cols_ref),
            )
        )
    ]
    for copy in smalls + fetches:
        copy.start()
    for copy in smalls:
        copy.wait()
    ids = (owners_ref[...] * PLACES + positions_ref[...]).astype(F32)
    for row, values in enumerate((ids, weights_ref[...])):
        note[pl.ds(row, BLOCK, stride=NOTES), :] = jnp.broadcast_to(values, (BLOCK, BLOCK))
    pairs = GROUP // NOTES
    copies = [
        pltpu.make_async_copy(
            note.reshape(BLOCK, 1, NOTES, BLOCK),
            o_ref.at[:, steps * pairs : steps * pairs + 1],
            sent.at[steps],
        )
    ]
    copies[0].start()
    prepare(coeffs_ref, weights_ref, rows_ref, cols_ref, rr, cc, scale)
    for t in range(steps):
        fetches[t].wait()
        spots = range(t * GROUP, (t + 1) * GROUP)
        out = filtered([held[b] for b in spots], spots, rr, cc, scale, lhs.at[t])
        spread(made.at[t], out)
        copies.append(
            pltpu.make_async_copy(
                made.at[t].reshape(BLOCK, pairs, NOTES, BLOCK),
                o_ref.at[:, t * pairs : (t + 1) * pairs],
                sent.at[t],
            )
        )
        copies[-1].start()
    for copy in copies:
        copy.wait()


def match_early(owners, positions, coeffs, weights, basis_rows, basis_cols, cutouts):
    whole = pl.BlockSpec(memory_space=pl.ANY)
    steps = FIRST // GROUP
    return pl.pallas_call(
        early_kernel,
        in_specs=[whole] * 7,
        out_specs=whole,
        out_shape=jax.ShapeDtypeStruct((BLOCK, FIRST // NOTES + 1, NOTES, BLOCK), F32),
        scratch_shapes=[
            pltpu.VMEM(x.shape, x.dtype)
            for x in (owners, positions, coeffs, weights, basis_rows, basis_cols)
        ]
        + [pltpu.SemaphoreType.DMA((6,))]
        + FILTER_SCRATCH[:3]
        + [
            pltpu.VMEM((steps, GROUP * BLOCK, 2 * TERMS * BLOCK), BF16),
            pltpu.VMEM((FIRST, BLOCK, BLOCK), F32),
            pltpu.VMEM((steps, BLOCK * GROUP, BLOCK), F32),
            pltpu.VMEM((BLOCK * NOTES, BLOCK), F32),
            pltpu.SemaphoreType.DMA((steps,)),
            pltpu.SemaphoreType.DMA((steps + 1,)),
        ],
        compiler_params=pltpu.CompilerParams(vmem_limit_bytes=VMEM),
    )(owners, positions, coeffs, weights, basis_rows, basis_cols, cutouts)


def match_kernel(order_ref, coeffs_ref, weights_ref, rows_ref, cols_ref, *refs):
    x_refs = refs[:GROUP]
    o_ref, rr, cc, scale, lhs = refs[GROUP:]
    step = pl.program_id(0)

    @pl.when(step == 0)
    def _():
        prepare(coeffs_ref, weights_ref, rows_ref, cols_ref, rr, cc, scale)

    spots = [order_ref[step * GROUP + b] for b in range(GROUP)]
    out = filtered([x[0] for x in x_refs], spots, rr, cc, scale, lhs)
    spread(o_ref.reshape(BLOCK * GROUP, BLOCK), out)


def match(order, coeffs, weights, basis_rows, basis_cols, cutouts):
    count = order.shape[0]
    vmem = pl.BlockSpec(memory_space=pltpu.VMEM)

    def pick(b):
        def block(i, order_ref):
            return (order_ref[i * GROUP + b], 0, 0)

        return pl.BlockSpec((1, BLOCK, BLOCK), block)

    return pl.pallas_call(
        match_kernel,
        grid_spec=pltpu.PrefetchScalarGridSpec(
            num_scalar_prefetch=1,
            grid=(count // GROUP,),
            in_specs=[vmem] * 4 + [pick(b) for b in range(GROUP)],
            out_specs=pl.BlockSpec((BLOCK, GROUP, BLOCK), lambda i, order_ref: (0, i, 0)),
            scratch_shapes=FILTER_SCRATCH,
        ),
        out_shape=jax.ShapeDtypeStruct((BLOCK, count, BLOCK), F32),
        compiler_params=pltpu.CompilerParams(vmem_limit_bytes=VMEM),
        cost_estimate=pl.CostEstimate(
            flops=count * 2 * 6 * TERMS * BLOCK**3,
            bytes_accessed=count * 8 * BLOCK * BLOCK,
            transcendentals=0,
        ),
    )(order, coeffs, weights, basis_rows, basis_cols, *[cutouts] * GROUP)


def combine_kernel(last, scalars_ref, ids_ref, x_ref, *refs):
    steps, _, depth = ids_ref.shape
    if last:
        prior_ref, o_ref, acc, held, got = refs
    else:
        o_ref, acc = refs

    def fetch(at):
        return pltpu.make_async_copy(
            x_ref.at[:, at * GROUP : (at + 1) * GROUP, :], held.at[at], got.at[at]
        )

    if last:
        for at in range(steps):
            fetch(at).start()
    acc[...] = prior_ref[...] if last else jnp.zeros_like(acc)
    wide = LATE_WIDE if last else WIDE
    spot = lax.broadcasted_iota(jnp.int32, (wide, depth), 0)
    for step in range(steps):
        if last:
            fetch(step).wait()
            rows = held[step].reshape(depth, BLOCK)
        else:
            peers = depth // GROUP
            rows = jnp.concatenate(
                [
                    x_ref[pl.ds(step * GROUP + b, peers, stride=FIRST + NOTES), :]
                    for b in range(GROUP)
                ],
                axis=0,
            )
        high, low = halves(rows)
        both = jnp.concatenate([high, low], axis=1)
        ids = ids_ref[step]

        def body(m, carry):
            at = pl.multiple_of(scalars_ref[1 + step] + m * wide, PLACES)
            near = (ids - at.astype(F32)).astype(jnp.int32)
            marks = jnp.where(spot == near, 1.0, 0.0).astype(BF16)
            sums = dot(marks, both)
            acc[pl.ds(at + PLACES, wide), :] += sums[:, :BLOCK] + sums[:, BLOCK:]
            return carry

        body(0, 0)
        lax.fori_loop(1, scalars_ref[1 + steps + step], body, 0)

    if not last:
        o_ref[...] = acc[...]
        return
    peers = o_ref.shape[0] // STRIPE
    for place in range(PLACES):
        o_ref[pl.ds(place, peers, stride=STRIPE), :] = acc[
            pl.ds(PLACES + place, peers, stride=PLACES), :
        ]
    for below in (False, True):

        @pl.when((scalars_ref[0] < BLOCK // 2) == below)
        def _():
            first = 2 * PLACES if below else PLACES - SIDE
            for c in range(SIDE):
                o_ref[pl.ds(PLACES + c, peers, stride=STRIPE), :] = acc[
                    pl.ds(first + c, peers, stride=PLACES), :
                ]


def combine(me, ids, rows, prior=None):
    last = prior is not None
    peers, count = ids.shape
    steps = count // GROUP
    depth = peers * GROUP
    tiles = ids.reshape(peers, steps, GROUP).transpose((1, 0, 2) if last else (1, 2, 0))
    base = jnp.min(tiles, axis=(1, 2)).astype(jnp.int32) // PLACES * PLACES
    turns = (jnp.max(tiles, axis=(1, 2)).astype(jnp.int32) - base) // (LATE_WIDE if last else WIDE) + 1
    room = PLACES + peers * PLACES + LATE_WIDE
    out = (peers * STRIPE if last else room, BLOCK)
    vmem = pl.BlockSpec(memory_space=pltpu.VMEM)
    return pl.pallas_call(
        functools.partial(combine_kernel, last),
        grid_spec=pltpu.PrefetchScalarGridSpec(
            num_scalar_prefetch=1,
            grid=(1,),
            in_specs=[vmem, pl.BlockSpec(memory_space=pl.ANY), vmem] if last else [vmem, vmem],
            out_specs=vmem,
            scratch_shapes=[pltpu.VMEM((room, BLOCK), F32)]
            + [
                pltpu.VMEM((steps, peers, GROUP, BLOCK), F32),
                pltpu.SemaphoreType.DMA((steps,)),
            ]
            * last,
        ),
        out_shape=jax.ShapeDtypeStruct(out, F32),
        compiler_params=pltpu.CompilerParams(vmem_limit_bytes=LEAN),
        cost_estimate=pl.CostEstimate(
            flops=4 * WIDE * steps * depth * BLOCK,
            bytes_accessed=steps * depth * BLOCK * 4,
            transcendentals=0,
        ),
    )(
        jnp.concatenate([me.reshape(1), base, turns]),
        tiles.reshape(steps, 1, depth),
        rows,
        *([prior] if last else []),
    )


def bands_kernel(taps_ref, down_ref, along_ref, row):
    row[...] = jnp.zeros_like(row)
    row[0:1, 0:TAPS] = taps_ref[...]
    taps = row[0:1, :]
    for part in range(2):
        high, low = halves(toeplitz(taps, HALF - EDGE + part * BLOCK))
        for copy, piece in enumerate((high, high, low)):
            at = (2 * copy + part) * BLOCK
            down_ref[:, at : at + BLOCK] = piece
    along_ref[...] = jnp.zeros_like(along_ref)
    for part in range(3):
        high, low = halves(toeplitz(taps, HALF + (part - 1) * BLOCK).T)
        for copy, piece in enumerate((high, high, low)):
            for half in range(2):
                at = copy * PATCH + (part + half) * BLOCK
                along_ref[at : at + BLOCK, half * BLOCK : (half + 1) * BLOCK] = piece


def make_bands(taps):
    vmem = pl.BlockSpec(memory_space=pltpu.VMEM)
    return pl.pallas_call(
        bands_kernel,
        in_specs=[vmem],
        out_specs=[vmem, vmem],
        out_shape=[
            jax.ShapeDtypeStruct((BLOCK, 6 * BLOCK), BF16),
            jax.ShapeDtypeStruct((3 * PATCH, 2 * BLOCK), BF16),
        ],
        scratch_shapes=[pltpu.VMEM((8, BLOCK), F32)],
        compiler_params=pltpu.CompilerParams(vmem_limit_bytes=LEAN),
    )(taps.reshape(1, TAPS))


def finish_kernel(
    divisor_ref,
    sums_ref,
    template_ref,
    above_ref,
    below_ref,
    down_ref,
    along_ref,
    coadd_out,
    detection_out,
    pad,
    row,
    coadd_ref,
    detection_ref,
    sent,
):
    flat = sums_ref
    spare = pad.shape[0] - PATCH - 2 * EDGE
    pad[2 * EDGE + PATCH :, :] = jnp.zeros((spare, PATCH), F32)
    row[:, :BLOCK] = jnp.zeros((PATCH, BLOCK), F32)
    row[:, BLOCK + PATCH :] = jnp.zeros((PATCH, BLOCK), F32)
    for c in range(SIDE):
        cols = slice(c * BLOCK, (c + 1) * BLOCK)
        numer = flat[pl.ds((BLOCK - EDGE) * STRIPE + PLACES + c, EDGE, stride=STRIPE), :]
        pad[:EDGE, cols] = (above_ref[:, cols] + numer) / divisor_ref[PLACES + c]
        numer = flat[pl.ds(PLACES + c, EDGE, stride=STRIPE), :]
        pad[EDGE + PATCH : 2 * EDGE + PATCH, cols] = (
            below_ref[:, cols] + numer
        ) / divisor_ref[PLACES + SIDE + c]
        for r in range(SIDE):
            place = r * SIDE + c
            numer = flat[pl.ds(place, BLOCK, stride=STRIPE), :]
            rows = slice(r * BLOCK, (r + 1) * BLOCK)
            made = (template_ref[rows, cols] + numer) / divisor_ref[place]
            coadd_ref[rows, cols] = made
            pad[EDGE + r * BLOCK : EDGE + (r + 1) * BLOCK, cols] = made
    coadd_copy = pltpu.make_async_copy(coadd_ref, coadd_out, sent.at[2])
    coadd_copy.start()
    for r in range(SIDE):
        high, low = halves(pad[r * BLOCK : (r + 2) * BLOCK, :])
        row[r * BLOCK : (r + 1) * BLOCK, BLOCK : BLOCK + PATCH] = dot(
            down_ref[...], jnp.concatenate([high, low, high], axis=0)
        )
    copies = []
    for h in range(2):
        high, low = halves(row[:, h * 2 * BLOCK : h * 2 * BLOCK + PATCH])
        cols = slice(h * 2 * BLOCK, (h + 1) * 2 * BLOCK)
        detection_ref[:, cols] = dot(jnp.concatenate([high, low, high], axis=1), along_ref[...])
        copies.append(
            pltpu.make_async_copy(detection_ref.at[:, cols], detection_out.at[:, cols], sent.at[h])
        )
        copies[-1].start()
    for copy in copies + [coadd_copy]:
        copy.wait()


def finish(divisor, sums, template, above, below, down, along):
    vmem = pl.BlockSpec(memory_space=pltpu.VMEM)
    image = jax.ShapeDtypeStruct((PATCH, PATCH), F32)
    return pl.pallas_call(
        finish_kernel,
        in_specs=[pl.BlockSpec(memory_space=pltpu.SMEM)] + [vmem] * 6,
        out_specs=[pl.BlockSpec(memory_space=pl.ANY)] * 2,
        out_shape=[image, image],
        scratch_shapes=[
            pltpu.VMEM((PATCH + BLOCK, PATCH), F32),
            pltpu.VMEM((PATCH, PATCH + 2 * BLOCK), F32),
            pltpu.VMEM((PATCH, PATCH), F32),
            pltpu.VMEM((PATCH, PATCH), F32),
            pltpu.SemaphoreType.DMA((3,)),
        ],
        compiler_params=pltpu.CompilerParams(vmem_limit_bytes=LEAN),
    )(divisor, sums, template, above, below, down, along)


def ranks(keys):
    before = jnp.arange(keys.shape[-1])
    before = before[None, :] < before[:, None]
    mine, other = keys[..., :, None], keys[..., None, :]
    return jnp.sum(((other < mine) | ((other == mine) & before)).astype(jnp.int32), axis=-1)


def argsorted(keys):
    spots = jnp.arange(keys.shape[-1], dtype=jnp.int32)
    hits = ranks(keys)[..., None, :] == spots[:, None]
    return jnp.sum(jnp.where(hits, spots, 0), axis=-1)


def in_order(keys):
    spots = jnp.arange(keys.shape[-1], dtype=jnp.int32)
    hits = ranks(keys)[..., None, :] == spots[:, None]
    return jnp.sum(jnp.where(hits, keys[..., None, :], 0.0), axis=-1)


def local(
    cutouts, coeffs, weights, owners, positions, basis_rows, basis_cols, template, detect_taps
):
    peers = lax.axis_size("sky")
    me = lax.axis_index("sky")
    blocks = cutouts.shape[0]
    given = (coeffs.T, weights.reshape(1, blocks), basis_rows, basis_cols, cutouts)
    early = match_early(owners.reshape(1, blocks), positions.reshape(1, blocks), *given)
    early = lax.all_to_all(early, "sky", split_axis=0, concat_axis=0, tiled=True)
    mine = owners[FIRST:, 0] * PLACES + positions[FIRST:]
    late = match(FIRST + argsorted(mine), *given)
    late = lax.all_to_all(late, "sky", split_axis=0, concat_axis=0, tiled=True)
    known, template_late = lax.optimization_barrier((early[:, -1], template))
    ids = known[:, 0, :]
    down, along = make_bands(detect_taps)
    above = lax.ppermute(
        template_late[PATCH - EDGE :], "sky", [(i, i + 1) for i in range(peers - 1)]
    )
    below = lax.ppermute(template_late[:EDGE], "sky", [(i + 1, i) for i in range(peers - 1)])
    wanted = jnp.concatenate(
        [
            jnp.arange(PLACES),
            jnp.arange(-SIDE, 0),
            jnp.arange(PLACES, PLACES + SIDE),
        ]
    )
    hits = ids[None] == (me * PLACES + wanted).astype(F32)[:, None, None]
    divisor = 1.0 + jnp.sum(jnp.where(hits, known[None, :, 1, :], 0.0), axis=(1, 2))
    sums = combine(me, ids[:, :FIRST], early.reshape(-1, BLOCK))
    late, sums, down, along, divisor, above, below = lax.optimization_barrier(
        (late, sums, down, along, divisor, above, below)
    )
    sums = combine(me, in_order(ids[:, FIRST:]), late, sums)
    sums = sums.reshape(peers, STRIPE // SIDE, SIDE, BLOCK)
    back = lax.all_to_all(sums, "sky", split_axis=0, concat_axis=0, tiled=True)
    back = back.reshape(peers * STRIPE, BLOCK)
    return tuple(finish(divisor, back, template, above, below, down, along))


def solution(mesh):
    placed = (
        P("sky", None, None),
        P("sky", None),
        P("sky"),
        P("sky", None),
        P("sky"),
        P(),
        P(),
        P("sky", None),
        P(),
    )
    return jax.shard_map(
        local,
        mesh=mesh,
        in_specs=placed,
        out_specs=(P("sky", None), P("sky", None)),
        check_vma=False,
    )
```

```python
import functools

import jax
import jax.numpy as jnp
from jax import lax
from jax.experimental import pallas as pl
from jax.experimental.pallas import tpu as pltpu
from jax.sharding import PartitionSpec as P

BLOCK = 128
SIDE = 4
PATCH = 512
PLACES = 16
TERMS = 3
TAPS = 41
HALF = 20
EDGE = 24
GROUP = 8
WIDE = 256
LATE_WIDE = 400
BATCHES = (2, 6, 16)
STRIPE = PLACES + SIDE
FIRST = 24
NOTES = 2
BANDS = ((0, 56, 0, 80), (56, 16, 32, 64), (72, 56, 48, 80))
VMEM = 56 * 1024 * 1024
LEAN = 24 * 1024 * 1024
F32 = jnp.float32
BF16 = jnp.bfloat16


def halves(x):
    high = x.astype(BF16)
    return high, (x - high.astype(F32)).astype(BF16)


def dot(a, b):
    return jnp.dot(a, b, preferred_element_type=F32)


def toeplitz(taps, offset):
    lane = lax.broadcasted_iota(jnp.int32, (BLOCK, BLOCK), 1)
    lag = lane - lax.broadcasted_iota(jnp.int32, (BLOCK, BLOCK), 0) + offset
    slant = pltpu.roll(jnp.broadcast_to(taps, (8, BLOCK)), 0, 1, stride=1, stride_axis=0)
    turned = jnp.concatenate(
        [pltpu.roll(slant, (at - offset) % BLOCK, 1) for at in range(0, BLOCK, 8)], axis=0
    )
    return jnp.where((lag >= 0) & (lag < TAPS), turned, 0.0)


def as_column(row):
    same = lax.broadcasted_iota(jnp.int32, (BLOCK, BLOCK), 0) == lax.broadcasted_iota(
        jnp.int32, (BLOCK, BLOCK), 1
    )
    return jnp.sum(jnp.where(same, row, jnp.zeros_like(row)), axis=1, keepdims=True)


def prepare(coeffs_ref, weights_ref, rows_ref, cols_ref, rr, cc, scale):
    wide = TERMS * BLOCK
    scale[0] = jnp.zeros((BLOCK, BLOCK), F32)
    scale[0, 0:TERMS, 0:TAPS] = rows_ref[...]
    scale[0, 8 : 8 + TERMS, 0:TAPS] = cols_ref[...]
    for k in range(TERMS):
        at = k * BLOCK
        high, low = halves(toeplitz(scale[0, k : k + 1, :], HALF))
        for first, count, start, reach in BANDS:
            into = TERMS * first + k * count
            picked = slice(first, first + count)
            seen = slice(start, start + reach)
            blank = jnp.zeros((count, 2 * BLOCK - 3 * reach), BF16)
            rr[into : into + count, :] = jnp.concatenate(
                [high[picked, seen], high[picked, seen], low[picked, seen], blank], axis=1
            )
        high, low = halves(toeplitz(scale[0, 8 + k : 9 + k, :], HALF).T)
        cc[at : at + BLOCK, :] = jnp.concatenate([high, low], axis=1)
        cc[wide + at : wide + at + BLOCK, :] = jnp.concatenate(
            [high, jnp.zeros_like(low)], axis=1
        )
    for k in range(TERMS):
        column = as_column(coeffs_ref[k : k + 1, :] * weights_ref[...])
        scale[k] = jnp.broadcast_to(column, (BLOCK, BLOCK))


def filtered(blocks, spots, rr, cc, scale, lhs):
    wide = TERMS * BLOCK
    for pair in range(GROUP // 2):
        high, low = halves(jnp.concatenate(blocks[2 * pair : 2 * pair + 2], axis=1))
        rowed = []
        for first, count, start, reach in BANDS:
            seen = slice(start, start + reach)
            spare = high[: 2 * BLOCK - 3 * reach]
            rowed.append(
                dot(
                    rr[TERMS * first : TERMS * (first + count), :],
                    jnp.concatenate([high[seen], low[seen], high[seen], spare], axis=0),
                )
            )
        for part in range(2):
            b = 2 * pair + part
            rows = slice(b * BLOCK, (b + 1) * BLOCK)
            for k in range(TERMS):
                piece = jnp.concatenate(
                    [
                        made[k * band[1] : (k + 1) * band[1], part * BLOCK : (part + 1) * BLOCK]
                        for made, band in zip(rowed, BANDS)
                    ],
                    axis=0,
                )
                upper, lower = halves(piece * scale[k, pl.ds(spots[b], 1), :])
                lhs[rows, k * BLOCK : (k + 1) * BLOCK] = upper
                lhs[rows, wide + k * BLOCK : wide + (k + 1) * BLOCK] = lower
    out = dot(lhs[...], cc[...])
    return out[:, :BLOCK] + out[:, BLOCK:]


def spread(flat, out):
    for b in range(GROUP):
        flat[pl.ds(b, BLOCK, stride=GROUP), :] = out[b * BLOCK : (b + 1) * BLOCK, :]


FILTER_SCRATCH = [
    pltpu.VMEM((TERMS * BLOCK, 2 * BLOCK), BF16),
    pltpu.VMEM((2 * TERMS * BLOCK, 2 * BLOCK), BF16),
    pltpu.VMEM((TERMS, BLOCK, BLOCK), F32),
    pltpu.VMEM((GROUP * BLOCK, 2 * TERMS * BLOCK), BF16),
]


def early_kernel(
    owners_in,
    positions_in,
    coeffs_in,
    weights_in,
    rows_in,
    cols_in,
    x_ref,
    o_ref,
    owners_ref,
    positions_ref,
    coeffs_ref,
    weights_ref,
    rows_ref,
    cols_ref,
    small,
    rr,
    cc,
    scale,
    lhs,
    held,
    made,
    note,
    got,
    sent,
):
    steps = FIRST // GROUP
    fetches = [
        pltpu.make_async_copy(
            x_ref.at[t * GROUP : (t + 1) * GROUP], held.at[t * GROUP : (t + 1) * GROUP], got.at[t]
        )
        for t in range(steps)
    ]
    smalls = [
        pltpu.make_async_copy(source, into, small.at[i])
        for i, (source, into) in enumerate(
            (
                (owners_in, owners_ref),
                (positions_in, positions_ref),
                (coeffs_in, coeffs_ref),
                (weights_in, weights_ref),
                (rows_in, rows_ref),
                (cols_in, cols_ref),
            )
        )
    ]
    for copy in smalls + fetches:
        copy.start()
    for copy in smalls:
        copy.wait()
    ids = (owners_ref[...] * PLACES + positions_ref[...]).astype(F32)
    for row, values in enumerate((ids, weights_ref[...])):
        note[pl.ds(row, BLOCK, stride=NOTES), :] = jnp.broadcast_to(values, (BLOCK, BLOCK))
    pairs = GROUP // NOTES
    copies = [
        pltpu.make_async_copy(
            note.reshape(BLOCK, 1, NOTES, BLOCK),
            o_ref.at[:, steps * pairs : steps * pairs + 1],
            sent.at[steps],
        )
    ]
    copies[0].start()
    prepare(coeffs_ref, weights_ref, rows_ref, cols_ref, rr, cc, scale)
    for copy in fetches:
        copy.wait()
    for t in range(steps):
        spots = range(t * GROUP, (t + 1) * GROUP)
        out = filtered([held[b] for b in spots], spots, rr, cc, scale, lhs.at[t])
        spread(made.at[t], out)
        copies.append(
            pltpu.make_async_copy(
                made.at[t].reshape(BLOCK, pairs, NOTES, BLOCK),
                o_ref.at[:, t * pairs : (t + 1) * pairs],
                sent.at[t],
            )
        )
        copies[-1].start()
    for copy in copies:
        copy.wait()


def match_early(owners, positions, coeffs, weights, basis_rows, basis_cols, cutouts):
    whole = pl.BlockSpec(memory_space=pl.ANY)
    steps = FIRST // GROUP
    return pl.pallas_call(
        early_kernel,
        in_specs=[whole] * 7,
        out_specs=whole,
        out_shape=jax.ShapeDtypeStruct((BLOCK, FIRST // NOTES + 1, NOTES, BLOCK), F32),
        scratch_shapes=[
            pltpu.VMEM(x.shape, x.dtype)
            for x in (owners, positions, coeffs, weights, basis_rows, basis_cols)
        ]
        + [pltpu.SemaphoreType.DMA((6,))]
        + FILTER_SCRATCH[:3]
        + [
            pltpu.VMEM((steps, GROUP * BLOCK, 2 * TERMS * BLOCK), BF16),
            pltpu.VMEM((FIRST, BLOCK, BLOCK), F32),
            pltpu.VMEM((steps, BLOCK * GROUP, BLOCK), F32),
            pltpu.VMEM((BLOCK * NOTES, BLOCK), F32),
            pltpu.SemaphoreType.DMA((steps,)),
            pltpu.SemaphoreType.DMA((steps + 1,)),
        ],
        compiler_params=pltpu.CompilerParams(vmem_limit_bytes=VMEM),
    )(owners, positions, coeffs, weights, basis_rows, basis_cols, cutouts)


def match_kernel(order_ref, coeffs_ref, weights_ref, rows_ref, cols_ref, *refs):
    x_refs = refs[:GROUP]
    o_ref, rr, cc, scale, lhs = refs[GROUP:]
    step = pl.program_id(0)

    @pl.when(step == 0)
    def _():
        prepare(coeffs_ref, weights_ref, rows_ref, cols_ref, rr, cc, scale)

    spots = [order_ref[step * GROUP + b] for b in range(GROUP)]
    out = filtered([x[0] for x in x_refs], spots, rr, cc, scale, lhs)
    spread(o_ref.reshape(BLOCK * GROUP, BLOCK), out)


def match(order, coeffs, weights, basis_rows, basis_cols, cutouts):
    count = order.shape[0]
    vmem = pl.BlockSpec(memory_space=pltpu.VMEM)

    def pick(b):
        def block(i, order_ref):
            return (order_ref[i * GROUP + b], 0, 0)

        return pl.BlockSpec((1, BLOCK, BLOCK), block)

    return pl.pallas_call(
        match_kernel,
        grid_spec=pltpu.PrefetchScalarGridSpec(
            num_scalar_prefetch=1,
            grid=(count // GROUP,),
            in_specs=[vmem] * 4 + [pick(b) for b in range(GROUP)],
            out_specs=pl.BlockSpec((BLOCK, GROUP, BLOCK), lambda i, order_ref: (0, i, 0)),
            scratch_shapes=FILTER_SCRATCH,
        ),
        out_shape=jax.ShapeDtypeStruct((BLOCK, count, BLOCK), F32),
        compiler_params=pltpu.CompilerParams(vmem_limit_bytes=VMEM),
        cost_estimate=pl.CostEstimate(
            flops=count * 2 * 6 * TERMS * BLOCK**3,
            bytes_accessed=count * 8 * BLOCK * BLOCK,
            transcendentals=0,
        ),
    )(order, coeffs, weights, basis_rows, basis_cols, *[cutouts] * GROUP)


def combine_kernel(last, scalars_ref, ids_ref, x_ref, *refs):
    steps, _, depth = ids_ref.shape
    if last:
        prior_ref, o_ref, acc, held, got = refs
    else:
        o_ref, acc = refs

    def fetch(at):
        return pltpu.make_async_copy(
            x_ref.at[:, at * GROUP : (at + 1) * GROUP, :], held.at[at], got.at[at]
        )

    if last:
        for at in range(steps):
            fetch(at).start()
    acc[...] = prior_ref[...] if last else jnp.zeros_like(acc)
    wide = LATE_WIDE if last else WIDE
    spot = lax.broadcasted_iota(jnp.int32, (wide, depth), 0)

    def add(step, m):
        if last:
            rows = held[step].reshape(depth, BLOCK)
        else:
            peers = depth // GROUP
            rows = jnp.concatenate(
                [
                    x_ref[pl.ds(step * GROUP + b, peers, stride=FIRST + NOTES), :]
                    for b in range(GROUP)
                ],
                axis=0,
            )
        high, low = halves(rows)
        at = pl.multiple_of(scalars_ref[1 + step] + m * wide, PLACES)
        near = (ids_ref[step] - at.astype(F32)).astype(jnp.int32)
        marks = jnp.where(spot == near, 1.0, 0.0).astype(BF16)
        sums = dot(marks, jnp.concatenate([high, low], axis=1))
        acc[pl.ds(at + PLACES, wide), :] += sums[:, :BLOCK] + sums[:, BLOCK:]

    begin = 0
    for end in BATCHES if last else (steps,):
        batch = range(begin, min(end, steps))
        if last:
            for step in batch:
                fetch(step).wait()
        for step in batch:
            add(step, 0)
        begin = end

    def rest(step, carry):
        def more(m, kept):
            add(step, m)
            return kept

        return lax.fori_loop(1, scalars_ref[1 + steps + step], more, carry)

    lax.fori_loop(0, steps, rest, 0)

    if not last:
        o_ref[...] = acc[...]
        return
    peers = o_ref.shape[0] // STRIPE
    for place in range(PLACES):
        o_ref[pl.ds(place, peers, stride=STRIPE), :] = acc[
            pl.ds(PLACES + place, peers, stride=PLACES), :
        ]
    for below in (False, True):

        @pl.when((scalars_ref[0] < BLOCK // 2) == below)
        def _():
            first = 2 * PLACES if below else PLACES - SIDE
            for c in range(SIDE):
                o_ref[pl.ds(PLACES + c, peers, stride=STRIPE), :] = acc[
                    pl.ds(first + c, peers, stride=PLACES), :
                ]


def combine(me, ids, rows, prior=None):
    last = prior is not None
    peers, count = ids.shape
    steps = count // GROUP
    depth = peers * GROUP
    tiles = ids.reshape(peers, steps, GROUP).transpose((1, 0, 2) if last else (1, 2, 0))
    base = jnp.min(tiles, axis=(1, 2)).astype(jnp.int32) // PLACES * PLACES
    turns = (jnp.max(tiles, axis=(1, 2)).astype(jnp.int32) - base) // (LATE_WIDE if last else WIDE) + 1
    room = PLACES + peers * PLACES + LATE_WIDE
    out = (peers * STRIPE if last else room, BLOCK)
    vmem = pl.BlockSpec(memory_space=pltpu.VMEM)
    return pl.pallas_call(
        functools.partial(combine_kernel, last),
        grid_spec=pltpu.PrefetchScalarGridSpec(
            num_scalar_prefetch=1,
            grid=(1,),
            in_specs=[vmem, pl.BlockSpec(memory_space=pl.ANY), vmem] if last else [vmem, vmem],
            out_specs=vmem,
            scratch_shapes=[pltpu.VMEM((room, BLOCK), F32)]
            + [
                pltpu.VMEM((steps, peers, GROUP, BLOCK), F32),
                pltpu.SemaphoreType.DMA((steps,)),
            ]
            * last,
        ),
        out_shape=jax.ShapeDtypeStruct(out, F32),
        compiler_params=pltpu.CompilerParams(vmem_limit_bytes=LEAN),
        cost_estimate=pl.CostEstimate(
            flops=4 * WIDE * steps * depth * BLOCK,
            bytes_accessed=steps * depth * BLOCK * 4,
            transcendentals=0,
        ),
    )(
        jnp.concatenate([me.reshape(1), base, turns]),
        tiles.reshape(steps, 1, depth),
        rows,
        *([prior] if last else []),
    )


def bands_kernel(taps_ref, down_ref, along_ref, row):
    row[...] = jnp.zeros_like(row)
    row[0:1, 0:TAPS] = taps_ref[...]
    taps = row[0:1, :]
    for part in range(2):
        high, low = halves(toeplitz(taps, HALF - EDGE + part * BLOCK))
        for copy, piece in enumerate((high, high, low)):
            at = (2 * copy + part) * BLOCK
            down_ref[:, at : at + BLOCK] = piece
    along_ref[...] = jnp.zeros_like(along_ref)
    for part in range(3):
        high, low = halves(toeplitz(taps, HALF + (part - 1) * BLOCK).T)
        for copy, piece in enumerate((high, high, low)):
            for half in range(2):
                at = copy * PATCH + (part + half) * BLOCK
                along_ref[at : at + BLOCK, half * BLOCK : (half + 1) * BLOCK] = piece


def make_bands(taps):
    vmem = pl.BlockSpec(memory_space=pltpu.VMEM)
    return pl.pallas_call(
        bands_kernel,
        in_specs=[vmem],
        out_specs=[vmem, vmem],
        out_shape=[
            jax.ShapeDtypeStruct((BLOCK, 6 * BLOCK), BF16),
            jax.ShapeDtypeStruct((3 * PATCH, 2 * BLOCK), BF16),
        ],
        scratch_shapes=[pltpu.VMEM((8, BLOCK), F32)],
        compiler_params=pltpu.CompilerParams(vmem_limit_bytes=LEAN),
    )(taps.reshape(1, TAPS))


def finish_kernel(
    divisor_ref,
    sums_ref,
    template_ref,
    above_ref,
    below_ref,
    down_ref,
    along_ref,
    coadd_out,
    detection_out,
    pad,
    row,
    coadd_ref,
    detection_ref,
    sent,
):
    flat = sums_ref
    spare = pad.shape[0] - PATCH - 2 * EDGE
    pad[2 * EDGE + PATCH :, :] = jnp.zeros((spare, PATCH), F32)
    row[:, :BLOCK] = jnp.zeros((PATCH, BLOCK), F32)
    row[:, BLOCK + PATCH :] = jnp.zeros((PATCH, BLOCK), F32)
    for c in range(SIDE):
        cols = slice(c * BLOCK, (c + 1) * BLOCK)
        numer = flat[pl.ds((BLOCK - EDGE) * STRIPE + PLACES + c, EDGE, stride=STRIPE), :]
        pad[:EDGE, cols] = (above_ref[:, cols] + numer) / divisor_ref[PLACES + c]
        numer = flat[pl.ds(PLACES + c, EDGE, stride=STRIPE), :]
        pad[EDGE + PATCH : 2 * EDGE + PATCH, cols] = (
            below_ref[:, cols] + numer
        ) / divisor_ref[PLACES + SIDE + c]
        for r in range(SIDE):
            place = r * SIDE + c
            numer = flat[pl.ds(place, BLOCK, stride=STRIPE), :]
            rows = slice(r * BLOCK, (r + 1) * BLOCK)
            made = (template_ref[rows, cols] + numer) / divisor_ref[place]
            coadd_ref[rows, cols] = made
            pad[EDGE + r * BLOCK : EDGE + (r + 1) * BLOCK, cols] = made
    coadd_copy = pltpu.make_async_copy(coadd_ref, coadd_out, sent.at[2])
    coadd_copy.start()
    for r in range(SIDE):
        high, low = halves(pad[r * BLOCK : (r + 2) * BLOCK, :])
        row[r * BLOCK : (r + 1) * BLOCK, BLOCK : BLOCK + PATCH] = dot(
            down_ref[...], jnp.concatenate([high, low, high], axis=0)
        )
    copies = []
    for h in range(2):
        high, low = halves(row[:, h * 2 * BLOCK : h * 2 * BLOCK + PATCH])
        cols = slice(h * 2 * BLOCK, (h + 1) * 2 * BLOCK)
        detection_ref[:, cols] = dot(jnp.concatenate([high, low, high], axis=1), along_ref[...])
        copies.append(
            pltpu.make_async_copy(detection_ref.at[:, cols], detection_out.at[:, cols], sent.at[h])
        )
        copies[-1].start()
    for copy in copies + [coadd_copy]:
        copy.wait()


def finish(divisor, sums, template, above, below, down, along):
    vmem = pl.BlockSpec(memory_space=pltpu.VMEM)
    image = jax.ShapeDtypeStruct((PATCH, PATCH), F32)
    return pl.pallas_call(
        finish_kernel,
        in_specs=[pl.BlockSpec(memory_space=pltpu.SMEM)] + [vmem] * 6,
        out_specs=[pl.BlockSpec(memory_space=pl.ANY)] * 2,
        out_shape=[image, image],
        scratch_shapes=[
            pltpu.VMEM((PATCH + BLOCK, PATCH), F32),
            pltpu.VMEM((PATCH, PATCH + 2 * BLOCK), F32),
            pltpu.VMEM((PATCH, PATCH), F32),
            pltpu.VMEM((PATCH, PATCH), F32),
            pltpu.SemaphoreType.DMA((3,)),
        ],
        compiler_params=pltpu.CompilerParams(vmem_limit_bytes=LEAN),
    )(divisor, sums, template, above, below, down, along)


def ranks(keys):
    before = jnp.arange(keys.shape[-1])
    before = before[None, :] < before[:, None]
    mine, other = keys[..., :, None], keys[..., None, :]
    return jnp.sum(((other < mine) | ((other == mine) & before)).astype(jnp.int32), axis=-1)


def argsorted(keys):
    spots = jnp.arange(keys.shape[-1], dtype=jnp.int32)
    hits = ranks(keys)[..., None, :] == spots[:, None]
    return jnp.sum(jnp.where(hits, spots, 0), axis=-1)


def in_order(keys):
    spots = jnp.arange(keys.shape[-1], dtype=jnp.int32)
    hits = ranks(keys)[..., None, :] == spots[:, None]
    return jnp.sum(jnp.where(hits, keys[..., None, :], 0.0), axis=-1)


def local(
    cutouts, coeffs, weights, owners, positions, basis_rows, basis_cols, template, detect_taps
):
    peers = lax.axis_size("sky")
    me = lax.axis_index("sky")
    blocks = cutouts.shape[0]
    given = (coeffs.T, weights.reshape(1, blocks), basis_rows, basis_cols, cutouts)
    early = match_early(owners.reshape(1, blocks), positions.reshape(1, blocks), *given)
    early = lax.all_to_all(early, "sky", split_axis=0, concat_axis=0, tiled=True)
    mine = owners[FIRST:, 0] * PLACES + positions[FIRST:]
    late = match(FIRST + argsorted(mine), *given)
    late = lax.all_to_all(late, "sky", split_axis=0, concat_axis=0, tiled=True)
    known, template_late = lax.optimization_barrier((early[:, -1], template))
    ids = known[:, 0, :]
    down, along = make_bands(detect_taps)
    above = lax.ppermute(
        template_late[PATCH - EDGE :], "sky", [(i, i + 1) for i in range(peers - 1)]
    )
    below = lax.ppermute(template_late[:EDGE], "sky", [(i + 1, i) for i in range(peers - 1)])
    wanted = jnp.concatenate(
        [
            jnp.arange(PLACES),
            jnp.arange(-SIDE, 0),
            jnp.arange(PLACES, PLACES + SIDE),
        ]
    )
    hits = ids[None] == (me * PLACES + wanted).astype(F32)[:, None, None]
    divisor = 1.0 + jnp.sum(jnp.where(hits, known[None, :, 1, :], 0.0), axis=(1, 2))
    sums = combine(me, ids[:, :FIRST], early.reshape(-1, BLOCK))
    late, sums, down, along, divisor, above, below = lax.optimization_barrier(
        (late, sums, down, along, divisor, above, below)
    )
    sums = combine(me, in_order(ids[:, FIRST:]), late, sums)
    sums = sums.reshape(peers, STRIPE // SIDE, SIDE, BLOCK)
    back = lax.all_to_all(sums, "sky", split_axis=0, concat_axis=0, tiled=True)
    back = back.reshape(peers * STRIPE, BLOCK)
    return tuple(finish(divisor, back, template, above, below, down, along))


def solution(mesh):
    placed = (
        P("sky", None, None),
        P("sky", None),
        P("sky"),
        P("sky", None),
        P("sky"),
        P(),
        P(),
        P("sky", None),
        P(),
    )
    return jax.shard_map(
        local,
        mesh=mesh,
        in_specs=placed,
        out_specs=(P("sky", None), P("sky", None)),
        check_vma=False,
    )
```

```python
import functools

import jax
import jax.numpy as jnp
from jax import lax
from jax.experimental import pallas as pl
from jax.experimental.pallas import tpu as pltpu
from jax.sharding import PartitionSpec as P

BLOCK = 128
SIDE = 4
PATCH = 512
PLACES = 16
TERMS = 3
TAPS = 41
HALF = 20
EDGE = 24
GROUP = 8
WIDE = 256
LATE_WIDE = 448
BATCHES = (2, 6, 16)
STRIPE = PLACES + SIDE
FIRST = 24
NOTES = 2
BANDS = ((0, 56, 0, 80), (56, 16, 32, 64), (72, 56, 48, 80))
VMEM = 56 * 1024 * 1024
LEAN = 24 * 1024 * 1024
F32 = jnp.float32
BF16 = jnp.bfloat16


def halves(x):
    high = x.astype(BF16)
    return high, (x - high.astype(F32)).astype(BF16)


def dot(a, b):
    return jnp.dot(a, b, preferred_element_type=F32)


def toeplitz(taps, offset):
    lane = lax.broadcasted_iota(jnp.int32, (BLOCK, BLOCK), 1)
    lag = lane - lax.broadcasted_iota(jnp.int32, (BLOCK, BLOCK), 0) + offset
    slant = pltpu.roll(jnp.broadcast_to(taps, (8, BLOCK)), 0, 1, stride=1, stride_axis=0)
    turned = jnp.concatenate(
        [pltpu.roll(slant, (at - offset) % BLOCK, 1) for at in range(0, BLOCK, 8)], axis=0
    )
    return jnp.where((lag >= 0) & (lag < TAPS), turned, 0.0)


def as_column(row):
    same = lax.broadcasted_iota(jnp.int32, (BLOCK, BLOCK), 0) == lax.broadcasted_iota(
        jnp.int32, (BLOCK, BLOCK), 1
    )
    return jnp.sum(jnp.where(same, row, jnp.zeros_like(row)), axis=1, keepdims=True)


def prepare(coeffs_ref, weights_ref, rows_ref, cols_ref, rr, cc, scale):
    wide = TERMS * BLOCK
    scale[0] = jnp.zeros((BLOCK, BLOCK), F32)
    scale[0, 0:TERMS, 0:TAPS] = rows_ref[...]
    scale[0, 8 : 8 + TERMS, 0:TAPS] = cols_ref[...]
    for k in range(TERMS):
        at = k * BLOCK
        high, low = halves(toeplitz(scale[0, k : k + 1, :], HALF))
        for first, count, start, reach in BANDS:
            into = TERMS * first + k * count
            picked = slice(first, first + count)
            seen = slice(start, start + reach)
            blank = jnp.zeros((count, 2 * BLOCK - 3 * reach), BF16)
            rr[into : into + count, :] = jnp.concatenate(
                [high[picked, seen], high[picked, seen], low[picked, seen], blank], axis=1
            )
        high, low = halves(toeplitz(scale[0, 8 + k : 9 + k, :], HALF).T)
        cc[at : at + BLOCK, :] = jnp.concatenate([high, low], axis=1)
        cc[wide + at : wide + at + BLOCK, :] = jnp.concatenate(
            [high, jnp.zeros_like(low)], axis=1
        )
    for k in range(TERMS):
        column = as_column(coeffs_ref[k : k + 1, :] * weights_ref[...])
        scale[k] = jnp.broadcast_to(column, (BLOCK, BLOCK))


def filtered(blocks, spots, rr, cc, scale, lhs):
    wide = TERMS * BLOCK
    for pair in range(GROUP // 2):
        high, low = halves(jnp.concatenate(blocks[2 * pair : 2 * pair + 2], axis=1))
        rowed = []
        for first, count, start, reach in BANDS:
            seen = slice(start, start + reach)
            spare = high[: 2 * BLOCK - 3 * reach]
            rowed.append(
                dot(
                    rr[TERMS * first : TERMS * (first + count), :],
                    jnp.concatenate([high[seen], low[seen], high[seen], spare], axis=0),
                )
            )
        for part in range(2):
            b = 2 * pair + part
            rows = slice(b * BLOCK, (b + 1) * BLOCK)
            for k in range(TERMS):
                piece = jnp.concatenate(
                    [
                        made[k * band[1] : (k + 1) * band[1], part * BLOCK : (part + 1) * BLOCK]
                        for made, band in zip(rowed, BANDS)
                    ],
                    axis=0,
                )
                upper, lower = halves(piece * scale[k, pl.ds(spots[b], 1), :])
                lhs[rows, k * BLOCK : (k + 1) * BLOCK] = upper
                lhs[rows, wide + k * BLOCK : wide + (k + 1) * BLOCK] = lower
    out = dot(lhs[...], cc[...])
    return out[:, :BLOCK] + out[:, BLOCK:]


def spread(flat, out):
    for b in range(GROUP):
        flat[pl.ds(b, BLOCK, stride=GROUP), :] = out[b * BLOCK : (b + 1) * BLOCK, :]


FILTER_SCRATCH = [
    pltpu.VMEM((TERMS * BLOCK, 2 * BLOCK), BF16),
    pltpu.VMEM((2 * TERMS * BLOCK, 2 * BLOCK), BF16),
    pltpu.VMEM((TERMS, BLOCK, BLOCK), F32),
    pltpu.VMEM((GROUP * BLOCK, 2 * TERMS * BLOCK), BF16),
]


def early_kernel(
    owners_in,
    positions_in,
    coeffs_in,
    weights_in,
    rows_in,
    cols_in,
    x_ref,
    o_ref,
    owners_ref,
    positions_ref,
    coeffs_ref,
    weights_ref,
    rows_ref,
    cols_ref,
    small,
    rr,
    cc,
    scale,
    lhs,
    held,
    made,
    note,
    got,
    sent,
):
    steps = FIRST // GROUP
    fetches = [
        pltpu.make_async_copy(
            x_ref.at[t * GROUP : (t + 1) * GROUP], held.at[t * GROUP : (t + 1) * GROUP], got.at[t]
        )
        for t in range(steps)
    ]
    smalls = [
        pltpu.make_async_copy(source, into, small.at[i])
        for i, (source, into) in enumerate(
            (
                (owners_in, owners_ref),
                (positions_in, positions_ref),
                (coeffs_in, coeffs_ref),
                (weights_in, weights_ref),
                (rows_in, rows_ref),
                (cols_in, cols_ref),
            )
        )
    ]
    for copy in smalls + fetches:
        copy.start()
    for copy in smalls:
        copy.wait()
    ids = (owners_ref[...] * PLACES + positions_ref[...]).astype(F32)
    for row, values in enumerate((ids, weights_ref[...])):
        note[pl.ds(row, BLOCK, stride=NOTES), :] = jnp.broadcast_to(values, (BLOCK, BLOCK))
    pairs = GROUP // NOTES
    copies = [
        pltpu.make_async_copy(
            note.reshape(BLOCK, 1, NOTES, BLOCK),
            o_ref.at[:, steps * pairs : steps * pairs + 1],
            sent.at[steps],
        )
    ]
    copies[0].start()
    prepare(coeffs_ref, weights_ref, rows_ref, cols_ref, rr, cc, scale)
    for copy in fetches:
        copy.wait()
    for t in range(steps):
        spots = range(t * GROUP, (t + 1) * GROUP)
        out = filtered([held[b] for b in spots], spots, rr, cc, scale, lhs.at[t])
        spread(made.at[t], out)
        copies.append(
            pltpu.make_async_copy(
                made.at[t].reshape(BLOCK, pairs, NOTES, BLOCK),
                o_ref.at[:, t * pairs : (t + 1) * pairs],
                sent.at[t],
            )
        )
        copies[-1].start()
    for copy in copies:
        copy.wait()


def match_early(owners, positions, coeffs, weights, basis_rows, basis_cols, cutouts):
    whole = pl.BlockSpec(memory_space=pl.ANY)
    steps = FIRST // GROUP
    return pl.pallas_call(
        early_kernel,
        in_specs=[whole] * 7,
        out_specs=whole,
        out_shape=jax.ShapeDtypeStruct((BLOCK, FIRST // NOTES + 1, NOTES, BLOCK), F32),
        scratch_shapes=[
            pltpu.VMEM(x.shape, x.dtype)
            for x in (owners, positions, coeffs, weights, basis_rows, basis_cols)
        ]
        + [pltpu.SemaphoreType.DMA((6,))]
        + FILTER_SCRATCH[:3]
        + [
            pltpu.VMEM((steps, GROUP * BLOCK, 2 * TERMS * BLOCK), BF16),
            pltpu.VMEM((FIRST, BLOCK, BLOCK), F32),
            pltpu.VMEM((steps, BLOCK * GROUP, BLOCK), F32),
            pltpu.VMEM((BLOCK * NOTES, BLOCK), F32),
            pltpu.SemaphoreType.DMA((steps,)),
            pltpu.SemaphoreType.DMA((steps + 1,)),
        ],
        compiler_params=pltpu.CompilerParams(vmem_limit_bytes=VMEM),
    )(owners, positions, coeffs, weights, basis_rows, basis_cols, cutouts)


def match_kernel(order_ref, coeffs_ref, weights_ref, rows_ref, cols_ref, *refs):
    x_refs = refs[:GROUP]
    o_ref, rr, cc, scale, lhs = refs[GROUP:]
    step = pl.program_id(0)

    @pl.when(step == 0)
    def _():
        prepare(coeffs_ref, weights_ref, rows_ref, cols_ref, rr, cc, scale)

    spots = [order_ref[step * GROUP + b] for b in range(GROUP)]
    out = filtered([x[0] for x in x_refs], spots, rr, cc, scale, lhs)
    spread(o_ref.reshape(BLOCK * GROUP, BLOCK), out)


def match(order, coeffs, weights, basis_rows, basis_cols, cutouts):
    count = order.shape[0]
    vmem = pl.BlockSpec(memory_space=pltpu.VMEM)

    def pick(b):
        def block(i, order_ref):
            return (order_ref[i * GROUP + b], 0, 0)

        return pl.BlockSpec((1, BLOCK, BLOCK), block)

    return pl.pallas_call(
        match_kernel,
        grid_spec=pltpu.PrefetchScalarGridSpec(
            num_scalar_prefetch=1,
            grid=(count // GROUP,),
            in_specs=[vmem] * 4 + [pick(b) for b in range(GROUP)],
            out_specs=pl.BlockSpec((BLOCK, GROUP, BLOCK), lambda i, order_ref: (0, i, 0)),
            scratch_shapes=FILTER_SCRATCH,
        ),
        out_shape=jax.ShapeDtypeStruct((BLOCK, count, BLOCK), F32),
        compiler_params=pltpu.CompilerParams(vmem_limit_bytes=VMEM),
        cost_estimate=pl.CostEstimate(
            flops=count * 2 * 6 * TERMS * BLOCK**3,
            bytes_accessed=count * 8 * BLOCK * BLOCK,
            transcendentals=0,
        ),
    )(order, coeffs, weights, basis_rows, basis_cols, *[cutouts] * GROUP)


def combine_kernel(last, scalars_ref, ids_ref, x_ref, *refs):
    steps, _, depth = ids_ref.shape
    if last:
        prior_ref, o_ref, acc, held, got = refs
    else:
        o_ref, acc = refs

    def fetch(at):
        return pltpu.make_async_copy(
            x_ref.at[:, at * GROUP : (at + 1) * GROUP, :], held.at[at], got.at[at]
        )

    if last:
        for at in range(steps):
            fetch(at).start()
    acc[...] = prior_ref[...] if last else jnp.zeros_like(acc)
    wide = LATE_WIDE if last else WIDE
    spot = lax.broadcasted_iota(jnp.int32, (wide, depth), 0)

    def add(step, m):
        if last:
            rows = held[step].reshape(depth, BLOCK)
        else:
            peers = depth // GROUP
            rows = jnp.concatenate(
                [
                    x_ref[pl.ds(step * GROUP + b, peers, stride=FIRST + NOTES), :]
                    for b in range(GROUP)
                ],
                axis=0,
            )
        high, low = halves(rows)
        at = pl.multiple_of(scalars_ref[1 + step] + m * wide, PLACES)
        near = (ids_ref[step] - at.astype(F32)).astype(jnp.int32)
        marks = jnp.where(spot == near, 1.0, 0.0).astype(BF16)
        sums = dot(marks, jnp.concatenate([high, low], axis=1))
        acc[pl.ds(at + PLACES, wide), :] += sums[:, :BLOCK] + sums[:, BLOCK:]

    begin = 0
    for end in BATCHES if last else (steps,):
        batch = range(begin, min(end, steps))
        if last:
            for step in batch:
                fetch(step).wait()
        for step in batch:
            add(step, 0)
        begin = end

    def rest(step, carry):
        def more(m, kept):
            add(step, m)
            return kept

        return lax.fori_loop(1, scalars_ref[1 + steps + step], more, carry)

    lax.fori_loop(0, steps, rest, 0)

    if not last:
        o_ref[...] = acc[...]
        return
    peers = o_ref.shape[0] // STRIPE
    for place in range(PLACES):
        o_ref[pl.ds(place, peers, stride=STRIPE), :] = acc[
            pl.ds(PLACES + place, peers, stride=PLACES), :
        ]
    for below in (False, True):

        @pl.when((scalars_ref[0] < BLOCK // 2) == below)
        def _():
            first = 2 * PLACES if below else PLACES - SIDE
            for c in range(SIDE):
                o_ref[pl.ds(PLACES + c, peers, stride=STRIPE), :] = acc[
                    pl.ds(first + c, peers, stride=PLACES), :
                ]


def combine(me, ids, rows, prior=None):
    last = prior is not None
    peers, count = ids.shape
    steps = count // GROUP
    depth = peers * GROUP
    tiles = ids.reshape(peers, steps, GROUP).transpose((1, 0, 2) if last else (1, 2, 0))
    base = jnp.min(tiles, axis=(1, 2)).astype(jnp.int32) // PLACES * PLACES
    turns = (jnp.max(tiles, axis=(1, 2)).astype(jnp.int32) - base) // (LATE_WIDE if last else WIDE) + 1
    room = PLACES + peers * PLACES + LATE_WIDE
    out = (peers * STRIPE if last else room, BLOCK)
    vmem = pl.BlockSpec(memory_space=pltpu.VMEM)
    return pl.pallas_call(
        functools.partial(combine_kernel, last),
        grid_spec=pltpu.PrefetchScalarGridSpec(
            num_scalar_prefetch=1,
            grid=(1,),
            in_specs=[vmem, pl.BlockSpec(memory_space=pl.ANY), vmem] if last else [vmem, vmem],
            out_specs=vmem,
            scratch_shapes=[pltpu.VMEM((room, BLOCK), F32)]
            + [
                pltpu.VMEM((steps, peers, GROUP, BLOCK), F32),
                pltpu.SemaphoreType.DMA((steps,)),
            ]
            * last,
        ),
        out_shape=jax.ShapeDtypeStruct(out, F32),
        compiler_params=pltpu.CompilerParams(vmem_limit_bytes=LEAN),
        cost_estimate=pl.CostEstimate(
            flops=4 * WIDE * steps * depth * BLOCK,
            bytes_accessed=steps * depth * BLOCK * 4,
            transcendentals=0,
        ),
    )(
        jnp.concatenate([me.reshape(1), base, turns]),
        tiles.reshape(steps, 1, depth),
        rows,
        *([prior] if last else []),
    )


def bands_kernel(taps_ref, down_ref, along_ref, row):
    row[...] = jnp.zeros_like(row)
    row[0:1, 0:TAPS] = taps_ref[...]
    taps = row[0:1, :]
    for part in range(2):
        high, low = halves(toeplitz(taps, HALF - EDGE + part * BLOCK))
        for copy, piece in enumerate((high, high, low)):
            at = (2 * copy + part) * BLOCK
            down_ref[:, at : at + BLOCK] = piece
    along_ref[...] = jnp.zeros_like(along_ref)
    for part in range(3):
        high, low = halves(toeplitz(taps, HALF + (part - 1) * BLOCK).T)
        for copy, piece in enumerate((high, high, low)):
            for half in range(2):
                at = copy * PATCH + (part + half) * BLOCK
                along_ref[at : at + BLOCK, half * BLOCK : (half + 1) * BLOCK] = piece


def make_bands(taps):
    vmem = pl.BlockSpec(memory_space=pltpu.VMEM)
    return pl.pallas_call(
        bands_kernel,
        in_specs=[vmem],
        out_specs=[vmem, vmem],
        out_shape=[
            jax.ShapeDtypeStruct((BLOCK, 6 * BLOCK), BF16),
            jax.ShapeDtypeStruct((3 * PATCH, 2 * BLOCK), BF16),
        ],
        scratch_shapes=[pltpu.VMEM((8, BLOCK), F32)],
        compiler_params=pltpu.CompilerParams(vmem_limit_bytes=LEAN),
    )(taps.reshape(1, TAPS))


def finish_kernel(
    divisor_ref,
    sums_ref,
    template_ref,
    above_ref,
    below_ref,
    down_ref,
    along_ref,
    coadd_out,
    detection_out,
    pad,
    row,
    coadd_ref,
    detection_ref,
    sent,
):
    flat = sums_ref
    spare = pad.shape[0] - PATCH - 2 * EDGE
    pad[2 * EDGE + PATCH :, :] = jnp.zeros((spare, PATCH), F32)
    row[:, :BLOCK] = jnp.zeros((PATCH, BLOCK), F32)
    row[:, BLOCK + PATCH :] = jnp.zeros((PATCH, BLOCK), F32)
    for c in range(SIDE):
        cols = slice(c * BLOCK, (c + 1) * BLOCK)
        numer = flat[pl.ds((BLOCK - EDGE) * STRIPE + PLACES + c, EDGE, stride=STRIPE), :]
        pad[:EDGE, cols] = (above_ref[:, cols] + numer) / divisor_ref[PLACES + c]
        numer = flat[pl.ds(PLACES + c, EDGE, stride=STRIPE), :]
        pad[EDGE + PATCH : 2 * EDGE + PATCH, cols] = (
            below_ref[:, cols] + numer
        ) / divisor_ref[PLACES + SIDE + c]
        for r in range(SIDE):
            place = r * SIDE + c
            numer = flat[pl.ds(place, BLOCK, stride=STRIPE), :]
            rows = slice(r * BLOCK, (r + 1) * BLOCK)
            made = (template_ref[rows, cols] + numer) / divisor_ref[place]
            coadd_ref[rows, cols] = made
            pad[EDGE + r * BLOCK : EDGE + (r + 1) * BLOCK, cols] = made
    coadd_copy = pltpu.make_async_copy(coadd_ref, coadd_out, sent.at[2])
    coadd_copy.start()
    for r in range(SIDE):
        high, low = halves(pad[r * BLOCK : (r + 2) * BLOCK, :])
        row[r * BLOCK : (r + 1) * BLOCK, BLOCK : BLOCK + PATCH] = dot(
            down_ref[...], jnp.concatenate([high, low, high], axis=0)
        )
    copies = []
    for h in range(2):
        high, low = halves(row[:, h * 2 * BLOCK : h * 2 * BLOCK + PATCH])
        cols = slice(h * 2 * BLOCK, (h + 1) * 2 * BLOCK)
        detection_ref[:, cols] = dot(jnp.concatenate([high, low, high], axis=1), along_ref[...])
        copies.append(
            pltpu.make_async_copy(detection_ref.at[:, cols], detection_out.at[:, cols], sent.at[h])
        )
        copies[-1].start()
    for copy in copies + [coadd_copy]:
        copy.wait()


def finish(divisor, sums, template, above, below, down, along):
    vmem = pl.BlockSpec(memory_space=pltpu.VMEM)
    image = jax.ShapeDtypeStruct((PATCH, PATCH), F32)
    return pl.pallas_call(
        finish_kernel,
        in_specs=[pl.BlockSpec(memory_space=pltpu.SMEM)] + [vmem] * 6,
        out_specs=[pl.BlockSpec(memory_space=pl.ANY)] * 2,
        out_shape=[image, image],
        scratch_shapes=[
            pltpu.VMEM((PATCH + BLOCK, PATCH), F32),
            pltpu.VMEM((PATCH, PATCH + 2 * BLOCK), F32),
            pltpu.VMEM((PATCH, PATCH), F32),
            pltpu.VMEM((PATCH, PATCH), F32),
            pltpu.SemaphoreType.DMA((3,)),
        ],
        compiler_params=pltpu.CompilerParams(vmem_limit_bytes=LEAN),
    )(divisor, sums, template, above, below, down, along)


def ranks(keys):
    before = jnp.arange(keys.shape[-1])
    before = before[None, :] < before[:, None]
    mine, other = keys[..., :, None], keys[..., None, :]
    return jnp.sum(((other < mine) | ((other == mine) & before)).astype(jnp.int32), axis=-1)


def argsorted(keys):
    spots = jnp.arange(keys.shape[-1], dtype=jnp.int32)
    hits = ranks(keys)[..., None, :] == spots[:, None]
    return jnp.sum(jnp.where(hits, spots, 0), axis=-1)


def in_order(keys):
    spots = jnp.arange(keys.shape[-1], dtype=jnp.int32)
    hits = ranks(keys)[..., None, :] == spots[:, None]
    return jnp.sum(jnp.where(hits, keys[..., None, :], 0.0), axis=-1)


def local(
    cutouts, coeffs, weights, owners, positions, basis_rows, basis_cols, template, detect_taps
):
    peers = lax.axis_size("sky")
    me = lax.axis_index("sky")
    blocks = cutouts.shape[0]
    given = (coeffs.T, weights.reshape(1, blocks), basis_rows, basis_cols, cutouts)
    early = match_early(owners.reshape(1, blocks), positions.reshape(1, blocks), *given)
    early = lax.all_to_all(early, "sky", split_axis=0, concat_axis=0, tiled=True)
    mine = owners[FIRST:, 0] * PLACES + positions[FIRST:]
    late = match(FIRST + argsorted(mine), *given)
    late = lax.all_to_all(late, "sky", split_axis=0, concat_axis=0, tiled=True)
    known, template_late = lax.optimization_barrier((early[:, -1], template))
    ids = known[:, 0, :]
    down, along = make_bands(detect_taps)
    above = lax.ppermute(
        template_late[PATCH - EDGE :], "sky", [(i, i + 1) for i in range(peers - 1)]
    )
    below = lax.ppermute(template_late[:EDGE], "sky", [(i + 1, i) for i in range(peers - 1)])
    wanted = jnp.concatenate(
        [
            jnp.arange(PLACES),
            jnp.arange(-SIDE, 0),
            jnp.arange(PLACES, PLACES + SIDE),
        ]
    )
    hits = ids[None] == (me * PLACES + wanted).astype(F32)[:, None, None]
    divisor = 1.0 + jnp.sum(jnp.where(hits, known[None, :, 1, :], 0.0), axis=(1, 2))
    sums = combine(me, ids[:, :FIRST], early.reshape(-1, BLOCK))
    late, sums, down, along, divisor, above, below = lax.optimization_barrier(
        (late, sums, down, along, divisor, above, below)
    )
    sums = combine(me, in_order(ids[:, FIRST:]), late, sums)
    sums = sums.reshape(peers, STRIPE // SIDE, SIDE, BLOCK)
    back = lax.all_to_all(sums, "sky", split_axis=0, concat_axis=0, tiled=True)
    back = back.reshape(peers * STRIPE, BLOCK)
    return tuple(finish(divisor, back, template, above, below, down, along))


def solution(mesh):
    placed = (
        P("sky", None, None),
        P("sky", None),
        P("sky"),
        P("sky", None),
        P("sky"),
        P(),
        P(),
        P("sky", None),
        P(),
    )
    return jax.shard_map(
        local,
        mesh=mesh,
        in_specs=placed,
        out_specs=(P("sky", None), P("sky", None)),
        check_vma=False,
    )
```
